32 devices in a mesh: ctx: 4 (over x, core), fsdp: 8 (over z, y).
Axes of the slice: x: 2, y: 2, z: 4, core: 2. Of those that a mesh axis runs over, the one named last changes fastest.
Arguments:
- inputs: bfloat16 [8, 512, 2048], P('fsdp', 'ctx'), may hold values from -6 to 6
- doc_starts: int32 [8, 512], P('fsdp'), may hold values from 0 to 1, as said below
- routes: int32 [8, 512, 8], P('fsdp', 'ctx'), may hold values from 0 to 23, all different within a row; in each aligned block of 128 rows (0 to 127, 128 to 255, ..., all dimensions but the last counted through in order) at most 53 rows name the same one
- gate_weights: float32 [8, 512, 8], P('fsdp', 'ctx'), may hold values from 0.04 to 0.25
- qkv_w: bfloat16 [2048, 3, 2048], P('fsdp'), may hold values from -0.125 to 0.125
- out_w: bfloat16 [2048, 2048], P('fsdp'), may hold values from -2 to 2
- norm_gains: bfloat16 [2048, 2], P('fsdp'), may hold values from 0.5 to 1.5
- head_gains: bfloat16 [128, 2], P('fsdp'), may hold values from 0.5 to 1.5
- gate_up: bfloat16 [2048, 24, 2048], P('ctx', 'fsdp'), may hold values from -0.125 to 0.125
- down_t: bfloat16 [2048, 24, 1024], P('ctx', 'fsdp'), may hold values from -0.75 to 0.75
- cotangent: bfloat16 [8, 512, 2048], P('fsdp', 'ctx'), may hold values from -6 to 6
Outputs:
- block_out: bfloat16 [8, 512, 2048], P('fsdp', 'ctx')
- inputs_grad: float32 [8, 512, 2048], P('fsdp', 'ctx')
- qkv_w_grad: float32 [2048, 3, 2048], P('fsdp')
- out_w_grad: float32 [2048, 2048], P('fsdp')
- norm_gains_grad: float32 [2048, 2], P('fsdp')
- head_gains_grad: float32 [128, 2], P('fsdp')
- gate_up_grad: float32 [2048, 24, 2048], P('ctx', 'fsdp')
- down_t_grad: float32 [2048, 24, 1024], P('ctx', 'fsdp')
The draws below stay inside these ranges and needn't reach their ends.
Inputs may be any that keep to these rules, and one draw needn't show every extreme that they name: `doc_starts`: 1 marks the first position of a document; position 0 of every stream is 1. `routes`: each row names 8 different experts; in the rows of one device no expert is named more than 53 times, a bound that some block reaches.
All inputs are finite; a program needn't handle non-finite values.
Results may differ from the reference program's by a relative error of at most 0.02.
Values may be sent and summed in bfloat16 or wider, within the bound.
No kernel may reach another device: no remote copies, remote signals or barrier semaphores. Data moves between devices by JAX's collectives and lax.ppermute only.
A program may use at most 384 MiB of HBM per device.

```python
import math
import jax
import jax.numpy as jnp
import numpy as np
from jax import lax

D = 2048
HEADS = 16
HD = 128
FF = 1024
TOPK = 8
TOK_DEV = 128
EXPERTS = 24
CAP = 53
STREAM_LEN = 512
STREAMS = 8
N_CTX = 4
N_FSDP = 8


def draw_doc_starts(key, part):
    stream_keys = jax.random.split(key, STREAMS)

    def one_stream(stream_key):
        first_key, last_key, mark_key = jax.random.split(stream_key, 3)
        places = jnp.arange(STREAM_LEN, dtype=jnp.int32)
        opening = jax.random.randint(first_key, (), 1, TOK_DEV)
        closing = jax.random.randint(last_key, (), STREAM_LEN - TOK_DEV + 1, STREAM_LEN)
        marks = jax.random.randint(mark_key, (STREAM_LEN,), 0, 24) == 0
        outside = (places < opening) | (places > closing)
        starts = (places == 0) | (places == opening) | (places == closing) | marks & outside
        return starts.astype(jnp.int32)
    return jax.vmap(one_stream)(stream_keys)


def levels(own_key, extent, cuts, least, top_value):
    loudness = 1.0
    for dim, shards_of in cuts:
        draws = jax.random.uniform(jax.random.fold_in(jax.random.fold_in(own_key, 6), dim), (shards_of,), jnp.float32, least / len(cuts), top_value / len(cuts))
        loudness = loudness * jnp.repeat(jnp.exp(draws), extent[dim] // shards_of).reshape((-1,) + (1,) * (len(extent) - 1 - dim))
    return loudness


def routed_block(key, own, number, rows, count, top, reach, slope):
    ranking = jax.random.permutation(key, count)
    packed, usual = load_shares(count, rows * top, reach, slope, True), load_shares(count, rows * top, reach, slope, False)
    places = jnp.arange(count)

    def named(sizes, offset_by):
        used = int((sizes > 0).sum())
        fixed = max(1, used // 4)
        moved = fixed + (places - fixed + offset_by * (used - fixed)) % max(1, count - fixed)
        return jnp.zeros((count,), jnp.int32).at[ranking[jnp.where(places < fixed, places, moved)]].set(jnp.asarray(sizes, jnp.int32))

    sizes = jnp.where(number % 4 == 0, named(packed, number // 4), named(usual, number - number // 4 - 1))
    mixed = jax.random.permutation(jax.random.fold_in(own, 3), count)
    source_of, receiver = mixed[0:count // 2 * 2:2], mixed[1:count // 2 * 2:2]
    room = jnp.minimum(sizes[source_of] - 1, reach - sizes[receiver]) // 2
    room = jnp.where((source_of == ranking[0]) | (receiver == ranking[0]) | (sizes[receiver] == 0), 0, jnp.maximum(room, 0))
    moved = jax.random.randint(jax.random.fold_in(own, 4), (count // 2,), 0, 1 << 20) % (room + 1)
    sizes = sizes.at[source_of].add(-moved).at[receiver].add(moved)
    items = jnp.searchsorted(jnp.cumsum(sizes), jnp.arange(rows * top), side="right").astype(jnp.int32)
    listing = items.reshape(top, rows).T
    listing = listing[jax.random.permutation(jax.random.fold_in(own, 1), rows)]
    offset_by = jax.random.randint(jax.random.fold_in(own, 2), (rows, 1), 0, top)
    return jnp.take_along_axis(listing, (jnp.arange(top)[None, :] + offset_by) % top, axis=1)


def load_shares(number_of, total, reach, lean, full):
    portions = [(1 << 20) // math.isqrt(rank ** lean) + 1 for rank in range(1, number_of + 1)]
    largest = reach if full else min(reach, max(-(-total // number_of), total * portions[0] // sum(portions)))
    least = 1 if total - largest >= number_of - 1 else 0
    counts, rest = [largest] + [least] * (number_of - 1), total - largest - least * (number_of - 1)
    while rest > 0:
        free = [i for i in range(1, number_of) if counts[i] < largest] or [i for i in range(1, number_of) if counts[i] < reach]
        mass, remaining = sum([portions[i] for i in free]), rest
        for i in free:
            extra = min(reach - counts[i], max(1, remaining * portions[i] // mass), rest)
            counts[i] = counts[i] + extra
            rest = rest - extra
    return np.array(counts)


def scatter_about(key, dims, spread, bound, cuts=(), held_as=jnp.bfloat16):
    array = spread * jax.random.normal(key, dims, jnp.float32)
    if cuts:
        array = array * levels(key, dims, cuts, -0.22, 0.18)
    return jnp.clip(array, -bound, bound).astype(held_as)


def setup_inputs(seed: int = 0) -> dict:
    key_of = jax.random.split(jax.random.key(seed), 12)
    inputs = scatter_about(key_of[0], (STREAMS, STREAM_LEN, D), 1.0, 6.0, ((0, 8), (1, 4)))
    doc_starts = draw_doc_starts(jax.random.fold_in(key_of[11], 71), 0)
    routes_keys = jax.random.split(jax.random.fold_in(key_of[2], 1), STREAMS * STREAM_LEN // TOK_DEV)
    routes_turns = jax.random.permutation(jax.random.fold_in(key_of[2], 3), STREAMS * STREAM_LEN // TOK_DEV)
    routes = jax.vmap(lambda own, number: routed_block(jax.random.fold_in(key_of[2], 2), own, number, TOK_DEV, EXPERTS, TOPK, CAP, 1))(routes_keys, routes_turns).reshape((STREAMS, STREAM_LEN, TOPK))
    gate_weights = jnp.clip(jnp.exp(math.log(0.25) - 1.8325815 * jax.random.uniform(key_of[3], (STREAMS, STREAM_LEN, TOPK), jnp.float32) ** levels(key_of[3], (STREAMS, STREAM_LEN, TOPK), ((0, 8), (1, 4)), -0.2, 0.2)), 0.04, 0.25)
    qkv_w = scatter_about(key_of[4], (D, 3, D), D ** -0.5, 0.125, ((0, 8),))
    out_w = scatter_about(key_of[5], (D, D), (max(D // 256, 1)) ** -0.5, 2.0, ((0, 8),))
    norm_gains = jnp.clip(1.0 + 0.1 * jax.random.normal(key_of[6], (D, 2), jnp.float32), 0.5, 1.5).astype(jnp.bfloat16)
    head_gains = jnp.clip(1.0 + 0.1 * jax.random.normal(key_of[7], (HD, 2), jnp.float32), 0.5, 1.5).astype(jnp.bfloat16)
    gate_up = scatter_about(key_of[8], (D, EXPERTS, 2 * FF), D ** -0.5, 0.125, ((0, 4), (1, 8)))
    down_t = scatter_about(key_of[9], (D, EXPERTS, FF), (FF // 16) ** -0.5, 0.75, ((0, 4), (1, 8)))
    cotangent = scatter_about(key_of[10], (STREAMS, STREAM_LEN, D), 1.0, 6.0, ((0, 8), (1, 4)))
    return {"inputs": inputs, "doc_starts": doc_starts, "routes": routes, "gate_weights": gate_weights, "qkv_w": qkv_w, "out_w": out_w, "norm_gains": norm_gains, "head_gains": head_gains, "gate_up": gate_up, "down_t": down_t, "cotangent": cotangent}


EPS = 1e-06
ROPE_BASE = 10000.0
HIGH = lax.Precision.HIGHEST

@jax.custom_vjp
def low(v):
    return lax.optimization_barrier(v.astype(jnp.bfloat16)).astype(jnp.float32)

@jax.custom_vjp
def low_back(v):
    return v

def low_keep(v):
    return (low(v), None)

def low_pass(kept, grad):
    return (grad,)

def back_keep(v):
    return (v, None)

def back_low(kept, grad):
    return (low(grad),)
low.defvjp(low_keep, low_pass)
low_back.defvjp(back_keep, back_low)

def rms_scale(values, gain):
    return values * lax.rsqrt(lax.optimization_barrier(jnp.mean(values * values, axis=-1, keepdims=True)) + EPS) * gain

def rotate(values, cosine, sine_part):
    half_dim = values.shape[-1] // 2
    first = values[..., :half_dim]
    second = values[..., half_dim:]
    return jnp.concatenate([first * cosine - second * sine_part, second * cosine + first * sine_part], axis=-1)

def doc_layout(doc_starts):
    length = doc_starts.shape[-1]
    places = jnp.arange(length, dtype=jnp.int32)
    marks = jnp.where(doc_starts == 1, places[None, :], jnp.zeros_like(doc_starts))
    begins = lax.cummax(marks, axis=1)
    doc_ids = jnp.cumsum(doc_starts, axis=1).astype(jnp.int32)
    return (doc_ids, (places[None, :] - begins).astype(jnp.int32))

def angles_of(relative):
    steps_half = jnp.arange(HD // 2, dtype=jnp.float32)
    frequency = jnp.exp(steps_half * (-2.0 / HD) * math.log(ROPE_BASE))
    angles = relative.astype(jnp.float32)[:, None] * frequency[None, :]
    return (jnp.cos(angles)[:, None, :], jnp.sin(angles)[:, None, :])

def attend_stream(a1_rows, doc_ids, relative, qkv_w, head_gains):
    length = a1_rows.shape[0]
    proj = low_back(jnp.einsum('td,djk->tjk', a1_rows, qkv_w, precision=HIGH))
    cosine, sine_part = angles_of(relative)
    q_heads = proj[:, 0].reshape(length, HEADS, HD)
    k_heads = proj[:, 1].reshape(length, HEADS, HD)
    q_rot = low(low_back(rotate(rms_scale(q_heads, head_gains[:, 0]), cosine, sine_part)))
    k_rot = low(low_back(rotate(rms_scale(k_heads, head_gains[:, 1]), cosine, sine_part)))
    v_low = low(proj[:, 2].reshape(length, HEADS, HD))
    query_width = min(512, length)
    block_count = length // query_width
    q_blocks = q_rot.reshape(block_count, query_width, HEADS, HD)
    doc_blocks = doc_ids.reshape(block_count, query_width)

    def query_block(pieces):
        q_block, doc_block = pieces
        logits = jnp.einsum('qhd,khd->hqk', q_block, k_rot, precision=HIGH) * HD ** (-0.5)
        logits = low_back(logits)
        same_doc = (doc_block[:, None] == doc_ids[None, :])[None]
        logits = jnp.where(same_doc, logits, -1e+30)
        attn_probs = jax.nn.softmax(logits, axis=-1)
        return jnp.einsum('hqk,khd->qhd', low(attn_probs), v_low, precision=HIGH)
    outputs = lax.map(jax.checkpoint(query_block), (q_blocks, doc_blocks))
    return low(low_back(outputs.reshape(length, HEADS * HD)))

def experts_apply(flat_rows, gate_up, down_t, routes, gate_weights):
    choices_flat = routes.reshape(-1)
    weights_flat = gate_weights.reshape(-1)
    capacity_all = CAP * N_CTX * N_FSDP

    def expert_step(running, pieces):
        expert_id, gate_up_e, down_e = pieces
        chosen = choices_flat == expert_id
        picked = jnp.nonzero(chosen, size=capacity_all, fill_value=0)[0].astype(jnp.int32)
        filled = jnp.arange(capacity_all) < jnp.sum(chosen)
        owners = (picked // TOPK).astype(jnp.int32)
        scaled = jnp.where(filled, weights_flat[picked], jnp.zeros_like(weights_flat[picked]))
        expert_in = low_back(flat_rows[owners])
        gate_pair = low_back(jnp.dot(expert_in, gate_up_e, precision=HIGH))
        hidden = low(jax.nn.silu(gate_pair[:, :FF]) * gate_pair[:, FF:])
        result = low(low_back(jnp.dot(hidden, down_e.T, precision=HIGH)))
        return (running.at[owners].add(scaled[:, None] * result), None)
    running, _ = lax.scan(jax.checkpoint(expert_step), jnp.zeros_like(flat_rows), (jnp.arange(EXPERTS, dtype=jnp.int32), jnp.transpose(gate_up, (1, 0, 2)), jnp.transpose(down_t, (1, 0, 2))))
    return running

def reference(inputs, doc_starts, routes, gate_weights, qkv_w, out_w, norm_gains, head_gains, gate_up, down_t, cotangent):
    doc_ids, relative = doc_layout(doc_starts)
    params = (inputs.astype(jnp.float32), qkv_w.astype(jnp.float32), out_w.astype(jnp.float32), norm_gains.astype(jnp.float32), head_gains.astype(jnp.float32), gate_up.astype(jnp.float32), down_t.astype(jnp.float32))

    def forward(weights):
        x_in, qkv_f, out_f, norm_f, head_f, gate_up_f, down_f = weights
        a1_all = low(rms_scale(x_in, norm_f[:, 0]))

        def stream_fn(pieces):
            return attend_stream(pieces[0], pieces[1], pieces[2], qkv_f, head_f)
        attn_low = lax.map(jax.checkpoint(stream_fn), (a1_all, doc_ids, relative))
        attn_out = low_back(jnp.einsum('std,dk->stk', attn_low, out_f, precision=HIGH))
        h_one = x_in + attn_out
        a2_all = low(rms_scale(h_one, norm_f[:, 1]))
        mixed = experts_apply(a2_all.reshape(-1, D), gate_up_f, down_f, routes, gate_weights)
        return h_one + mixed.reshape(h_one.shape)
    primal, backward = jax.vjp(forward, params)
    grads = backward(cotangent.astype(jnp.float32))[0]
    return (primal.astype(jnp.bfloat16), grads[0], grads[1], grads[2], grads[3], grads[4], grads[5], grads[6])
```

```python
import math

import jax
import jax.numpy as jnp
from jax import lax
from jax.sharding import PartitionSpec as P

EPS = 1e-06
ROPE_BASE = 10000.0
NEG_FILL = -1e30
f32 = jnp.float32
bf16 = jnp.bfloat16


def rms_scale(values, gain):
    return values * lax.rsqrt(jnp.mean(values * values, axis=-1, keepdims=True) + EPS) * gain


def rotate(values, cosine, sine_part):
    half_dim = values.shape[-1] // 2
    first = values[..., :half_dim]
    second = values[..., half_dim:]
    return jnp.concatenate(
        [first * cosine - second * sine_part, second * cosine + first * sine_part], axis=-1
    )


def swap(value, axis, mask):
    size = lax.axis_size(axis)
    return lax.ppermute(value, axis, [(i, i ^ mask) for i in range(size)])


def bits_down(size):
    return [1 << b for b in reversed(range(size.bit_length() - 1))]


def gather_ctx(block):
    pieces = {0: block}
    for bit in bits_down(lax.axis_size("ctx")):
        pieces.update({q | bit: swap(piece, "ctx", bit) for q, piece in list(pieces.items())})
    return [pieces[q] for q in range(len(pieces))]


def scatter_ctx(blocks):
    size = lax.axis_size("ctx")
    current = dict(enumerate(blocks))
    for bit in reversed(bits_down(size)):
        current = {
            q: current[q].astype(f32) + swap(current[q | bit].astype(bf16), "ctx", bit).astype(f32)
            for q in current
            if not q & bit
        }
    return current[0]


def gather_fsdp(block):
    size = lax.axis_size("fsdp")
    even = {0: block}
    even.update({m: swap(block, "fsdp", m) for m in range(2, size, 2)})
    out = [None] * size
    for q, piece in even.items():
        out[q] = piece
        out[q | 1] = swap(piece, "fsdp", 1)
    return out


def scatter_fsdp(blocks):
    size = lax.axis_size("fsdp")
    even = {
        q: blocks[q].astype(f32) + swap(blocks[q | 1].astype(bf16), "fsdp", 1).astype(f32)
        for q in range(0, size, 2)
    }
    total = even[0]
    for m in range(2, size, 2):
        total = total + swap(even[m].astype(bf16), "fsdp", m).astype(f32)
    return total


def xor_blocks(values, index, count):
    shape = values.shape
    width = shape[-1] // count
    for bit in bits_down(count):
        parts = values.reshape(shape[:-1] + (count // (2 * bit), 2, bit * width))
        flipped = jnp.concatenate([parts[..., 1:, :], parts[..., :1, :]], axis=-2)
        values = jnp.where((index & bit) != 0, flipped, parts).reshape(shape)
    return values


def body(
    inputs,
    doc_starts,
    routes,
    gate_weights,
    qkv_w,
    out_w,
    norm_gains,
    head_gains,
    gate_up,
    down_t,
    cotangent,
):
    n_ctx, n_fsdp = lax.axis_size("ctx"), lax.axis_size("fsdp")
    c, f = lax.axis_index("ctx"), lax.axis_index("fsdp")
    tok_rows, model_width = inputs.shape[1:]
    head_dim = head_gains.shape[0] * n_fsdp
    own_width = model_width // n_ctx
    own_heads = own_width // head_dim
    score_scale = head_dim ** (-0.5)
    top_count = routes.shape[2]
    hidden_units = down_t.shape[2]
    local_experts = gate_up.shape[1]
    experts_all = local_experts * n_fsdp
    capacity = tok_rows * top_count * 5 // (experts_all * 4)
    slots = n_fsdp * capacity
    stream_len = doc_starts.shape[1]
    half_dim = head_dim // 2

    x_low = inputs[0]
    x_rows = x_low.astype(f32)
    cot_low = cotangent[0]
    cot_rows = cot_low.astype(f32)

    x_all = jnp.concatenate(gather_ctx(xor_blocks(x_low, f, n_fsdp)), axis=0)
    qkv_own = lax.dynamic_slice_in_dim(qkv_w, c * own_width, own_width, axis=2)
    qkv_all = jnp.concatenate(gather_fsdp(qkv_own), axis=0)
    units = n_ctx * n_fsdp
    out_piece_rows = out_w.shape[0] // n_ctx
    flat = lambda ci, fi: ci * n_fsdp + fi
    to_heads = [(flat(u % n_ctx, u // n_ctx), flat(u // n_fsdp, u % n_fsdp)) for u in range(units)]
    out_piece = lax.ppermute(
        lax.dynamic_slice_in_dim(out_w, c * out_piece_rows, out_piece_rows, axis=0),
        ("ctx", "fsdp"),
        to_heads,
    )
    out_pieces = gather_fsdp(out_piece)
    out_own = jnp.zeros((own_width, model_width), bf16)
    for q, piece in enumerate(out_pieces):
        out_own = lax.dynamic_update_slice_in_dim(out_own, piece, (f ^ q) * out_piece_rows, axis=0)

    gains = lax.all_gather(
        jnp.concatenate([norm_gains, head_gains], axis=0).T, "fsdp", axis=0
    ).astype(f32)
    norm_one = gains[:, 0, : norm_gains.shape[0]].reshape(model_width)
    norm_two = gains[:, 1, : norm_gains.shape[0]].reshape(model_width)
    head_q = gains[:, 0, norm_gains.shape[0] :].reshape(head_dim)
    head_k = gains[:, 1, norm_gains.shape[0] :].reshape(head_dim)

    cot_all = jnp.concatenate(gather_fsdp(xor_blocks(cot_low, c, n_ctx)), axis=0)
    gate_up_all = [
        jnp.concatenate(gather_ctx(gate_up[:, e, :]), axis=0) for e in range(local_experts)
    ]
    down_all = [jnp.concatenate(gather_ctx(down_t[:, e, :]), axis=0) for e in range(local_experts)]

    places = jnp.arange(stream_len, dtype=jnp.int32)
    spots = ((c ^ (places // tok_rows)) * tok_rows + places % tok_rows).astype(jnp.int32)
    starts = doc_starts[0]
    reach = spots[:, None] >= places[None, :]
    doc_ids = jnp.sum(jnp.where(reach, starts[None, :], 0), axis=1)
    begins = jnp.max(jnp.where(reach & (starts[None, :] == 1), places[None, :], 0), axis=1)
    relative = spots - begins
    same_doc = (doc_ids[:, None] == doc_ids[None, :])[None]
    frequency = jnp.exp(jnp.arange(half_dim, dtype=f32) * (-2.0 / head_dim) * math.log(ROPE_BASE))
    angles = relative.astype(f32)[:, None] * frequency[None, :]
    cosine = jnp.cos(angles)[:, None, :]
    sine_part = jnp.sin(angles)[:, None, :]

    a1 = rms_scale(x_all.astype(f32), xor_blocks(norm_one, f, n_fsdp)).astype(bf16)
    proj = jnp.einsum("td,djk->tjk", a1, qkv_all, preferred_element_type=f32)

    def prepare(q_flat, k_flat, q_gain, k_gain):
        q_heads = rms_scale(q_flat.reshape(stream_len, own_heads, head_dim), q_gain)
        k_heads = rms_scale(k_flat.reshape(stream_len, own_heads, head_dim), k_gain)
        return (rotate(q_heads, cosine, sine_part), rotate(k_heads, cosine, sine_part))

    (q_rot, k_rot), prepare_back = jax.vjp(prepare, proj[:, 0], proj[:, 1], head_q, head_k)
    q_low = q_rot.astype(bf16)
    k_low = k_rot.astype(bf16)
    v_low = proj[:, 2].reshape(stream_len, own_heads, head_dim).astype(bf16)
    logits = jnp.einsum("qhd,khd->hqk", q_low, k_low, preferred_element_type=f32) * score_scale
    logits = jnp.where(same_doc, logits, NEG_FILL)
    probs = jax.nn.softmax(logits, axis=-1)
    probs_low = probs.astype(bf16)
    attn_acc = jnp.einsum("hqk,khd->qhd", probs_low, v_low, preferred_element_type=f32)
    attn_low = attn_acc.reshape(stream_len, own_width).astype(bf16)
    mixed_heads = jnp.dot(attn_low, out_own, preferred_element_type=f32).astype(bf16)
    h_one = x_rows + scatter_ctx(
        [mixed_heads[q * tok_rows : (q + 1) * tok_rows] for q in range(n_ctx)]
    )
    a2_f32, norm_two_back = jax.vjp(rms_scale, h_one, norm_two)
    a2_low = a2_f32.astype(bf16)
    a2_all = jnp.concatenate(gather_fsdp(xor_blocks(a2_low, c, n_ctx)), axis=0)

    tokens = n_fsdp * tok_rows
    routed = lax.all_gather(
        jnp.concatenate([routes[0].astype(f32), gate_weights[0]], axis=1).T, "fsdp", axis=0
    )
    routed = xor_blocks(
        routed.transpose(1, 0, 2).reshape(2 * top_count, tokens), f, n_fsdp
    )
    own = (f * local_experts + jnp.arange(local_experts, dtype=jnp.int32)).astype(f32)
    chosen = routed[None, :top_count] == own[:, None, None]
    member = jnp.any(chosen, axis=1)
    weight = jnp.sum(jnp.where(chosen, routed[None, top_count:], 0.0), axis=1)
    token_ids = jnp.arange(tokens, dtype=jnp.int32)
    before = (token_ids[:, None] < token_ids[None, :]).astype(bf16)
    rank = jnp.dot(member.astype(bf16), before, preferred_element_type=f32).astype(jnp.int32)
    place = jnp.where(member, rank, -1)
    picks = place[:, None, :] == jnp.arange(slots, dtype=jnp.int32)[None, :, None]
    slot_weight = jnp.sum(jnp.where(picks, weight[:, None, :], 0.0), axis=2)
    picks = picks.astype(bf16)

    made, made_grads, gate_up_grads, down_grads = [], [], [], []
    for e in range(local_experts):
        rows = jnp.dot(picks[e], a2_all, preferred_element_type=f32).astype(bf16)
        scale = slot_weight[e][:, None]
        dy = (scale * jnp.dot(picks[e], cot_all, preferred_element_type=f32)).astype(bf16)
        gate_w = gate_up_all[e]
        gate_add = jnp.dot(rows, gate_w[:, :hidden_units], preferred_element_type=f32)
        up_add = jnp.dot(rows, gate_w[:, hidden_units:], preferred_element_type=f32)
        hidden_grad = jnp.dot(dy, down_all[e], preferred_element_type=f32)
        sigmoid_g = jax.nn.sigmoid(gate_add)
        activated = gate_add * sigmoid_g
        hidden_low = (activated * up_add).astype(bf16)
        gate_grad = (hidden_grad * up_add * sigmoid_g * (1.0 + gate_add * (1.0 - sigmoid_g))).astype(
            bf16
        )
        up_grad = (hidden_grad * activated).astype(bf16)
        pair_grad = jnp.concatenate([gate_grad, up_grad], axis=1)
        y_rows = jnp.einsum("rf,df->rd", hidden_low, down_all[e], preferred_element_type=f32)
        made.append((scale * y_rows.astype(bf16).astype(f32)).astype(bf16))
        made_grads.append(
            jnp.einsum("rk,dk->rd", pair_grad, gate_w, preferred_element_type=f32).astype(bf16)
        )
        pair_part = jnp.einsum("rd,rk->dk", rows, pair_grad, preferred_element_type=f32)
        down_part = jnp.einsum("rd,rf->df", dy, hidden_low, preferred_element_type=f32)
        blocks = [slice(p * own_width, (p + 1) * own_width) for p in range(n_ctx)]
        gate_up_grads.append(scatter_ctx([pair_part[b].astype(bf16) for b in blocks]))
        down_grads.append(scatter_ctx([down_part[b].astype(bf16) for b in blocks]))

    grads_back = jnp.einsum("est,esd->td", picks, jnp.stack(made_grads), preferred_element_type=f32)
    grads_back = grads_back.astype(bf16).reshape(n_fsdp, tok_rows, model_width)
    da2 = xor_blocks(scatter_fsdp([grads_back[q] for q in range(n_fsdp)]), c, n_ctx)
    mixed = jnp.einsum("est,esd->td", picks, jnp.stack(made), preferred_element_type=f32)
    mixed = mixed.astype(bf16).reshape(n_fsdp, tok_rows, model_width)
    mixed = xor_blocks(scatter_fsdp([mixed[q] for q in range(n_fsdp)]), c, n_ctx)
    block_out = (h_one + mixed).astype(bf16)

    dh_part, gain_two_grad = norm_two_back(da2)
    dh_one = cot_rows + dh_part
    dattn = jnp.concatenate(gather_ctx(dh_one.astype(bf16)), axis=0)
    d_out = jnp.einsum("tk,dk->td", dattn, out_own, preferred_element_type=f32)
    d_out = d_out.astype(bf16).reshape(stream_len, own_heads, head_dim)
    prob_grad = jnp.einsum("qhd,khd->hqk", d_out, v_low, preferred_element_type=f32)
    row_delta = jnp.sum(probs * prob_grad, axis=2, keepdims=True)
    logit_grad = (probs * (prob_grad - row_delta)).astype(bf16)
    dq = jnp.einsum("hqk,khd->qhd", logit_grad, k_low, preferred_element_type=f32) * score_scale
    dk = jnp.einsum("hqk,qhd->khd", logit_grad, q_low, preferred_element_type=f32) * score_scale
    dv = jnp.einsum("hqk,qhd->khd", probs_low, d_out, preferred_element_type=f32)
    dq_proj, dk_proj, q_gain_grad, k_gain_grad = prepare_back(
        (dq.astype(bf16).astype(f32), dk.astype(bf16).astype(f32))
    )
    proj_grad = jnp.stack([dq_proj, dk_proj, dv.reshape(stream_len, own_width)], axis=1).astype(bf16)
    da1 = jnp.einsum("tjk,djk->td", proj_grad, qkv_all, preferred_element_type=f32).astype(bf16)
    da1 = scatter_ctx([da1[q * tok_rows : (q + 1) * tok_rows] for q in range(n_ctx)])
    da1 = xor_blocks(da1, f, n_fsdp)
    _, norm_one_back = jax.vjp(rms_scale, x_rows, norm_one)
    dx_part, gain_one_grad = norm_one_back(da1)
    inputs_grad = dh_one + dx_part

    qkv_part = jnp.einsum("td,tjk->djk", a1, proj_grad, preferred_element_type=f32).astype(bf16)
    row_count = qkv_w.shape[0]
    qkv_sum = scatter_fsdp([qkv_part[q * row_count : (q + 1) * row_count] for q in range(n_fsdp)])
    out_part = jnp.einsum("td,tk->dk", attn_low, dattn, preferred_element_type=f32).astype(bf16)
    out_sum = scatter_fsdp(
        [
            lax.dynamic_slice_in_dim(out_part, (f ^ q) * out_piece_rows, out_piece_rows, axis=0)
            for q in range(n_fsdp)
        ]
    )
    qkv_grad = jnp.zeros((row_count, 3, model_width), f32)
    for q, piece in enumerate(gather_ctx(qkv_sum.astype(bf16))):
        qkv_grad = lax.dynamic_update_slice_in_dim(
            qkv_grad, piece.astype(f32), (c ^ q) * own_width, axis=2
        )
    out_sum = lax.ppermute(out_sum.astype(bf16), ("ctx", "fsdp"), [(b, a) for a, b in to_heads])
    out_grad = jnp.zeros((row_count, model_width), f32)
    for q, piece in enumerate(gather_ctx(out_sum)):
        out_grad = lax.dynamic_update_slice_in_dim(
            out_grad, piece.astype(f32), (c ^ q) * out_piece_rows, axis=0
        )

    gain_sums = lax.psum(
        jnp.concatenate(
            [
                jnp.stack([gain_one_grad, gain_two_grad]),
                jnp.stack([q_gain_grad, k_gain_grad]),
            ],
            axis=1,
        ),
        ("ctx", "fsdp"),
    )
    norm_rows = norm_gains.shape[0]
    norm_grad = lax.dynamic_slice_in_dim(gain_sums, f * norm_rows, norm_rows, axis=1).T
    head_rows = head_gains.shape[0]
    head_grad = lax.dynamic_slice_in_dim(
        gain_sums, model_width + f * head_rows, head_rows, axis=1
    ).T
    return (
        block_out[None],
        inputs_grad[None],
        qkv_grad,
        out_grad,
        norm_grad,
        head_grad,
        jnp.stack(gate_up_grads, axis=1),
        jnp.stack(down_grads, axis=1),
    )


def solution(mesh):
    return jax.shard_map(
        body,
        mesh=mesh,
        in_specs=(
            P("fsdp", "ctx", None),
            P("fsdp", None),
            P("fsdp", "ctx", None),
            P("fsdp", "ctx", None),
            P("fsdp", None, None),
            P("fsdp", None),
            P("fsdp", None),
            P("fsdp", None),
            P("ctx", "fsdp", None),
            P("ctx", "fsdp", None),
            P("fsdp", "ctx", None),
        ),
        out_specs=(
            P("fsdp", "ctx", None),
            P("fsdp", "ctx", None),
            P("fsdp", None, None),
            P("fsdp", None),
            P("fsdp", None),
            P("fsdp", None),
            P("ctx", "fsdp", None),
            P("ctx", "fsdp", None),
        ),
        check_vma=False,
    )
```

```python
import math

import jax
import jax.numpy as jnp
import numpy as np
from jax import lax
from jax.experimental import pallas as pl
from jax.experimental.pallas import tpu as pltpu
from jax.sharding import PartitionSpec as P

EPS = 1e-06
ROPE_BASE = 10000.0
NEG_FILL = -1e30
f32 = jnp.float32
bf16 = jnp.bfloat16


def rms_scale(values, gain):
    return values * lax.rsqrt(jnp.mean(values * values, axis=-1, keepdims=True) + EPS) * gain


def rotate(values, cosine, sine_part):
    half_dim = values.shape[-1] // 2
    first = values[..., :half_dim]
    second = values[..., half_dim:]
    return jnp.concatenate(
        [first * cosine - second * sine_part, second * cosine + first * sine_part], axis=-1
    )


def swap(value, axis, mask):
    size = lax.axis_size(axis)
    return lax.ppermute(value, axis, [(i, i ^ mask) for i in range(size)])


def bits_down(size):
    return [1 << b for b in reversed(range(size.bit_length() - 1))]


def gather_ctx(block):
    pieces = {0: block}
    for bit in bits_down(lax.axis_size("ctx")):
        pieces.update({q | bit: swap(piece, "ctx", bit) for q, piece in list(pieces.items())})
    return [pieces[q] for q in range(len(pieces))]


def scatter_ctx(blocks):
    size = lax.axis_size("ctx")
    current = dict(enumerate(blocks))
    for bit in reversed(bits_down(size)):
        current = {
            q: current[q].astype(f32) + swap(current[q | bit].astype(bf16), "ctx", bit).astype(f32)
            for q in current
            if not q & bit
        }
    return current[0]


def gather_fsdp(block):
    size = lax.axis_size("fsdp")
    even = {0: block}
    even.update({m: swap(block, "fsdp", m) for m in range(2, size, 2)})
    out = [None] * size
    for q, piece in even.items():
        out[q] = piece
        out[q | 1] = swap(piece, "fsdp", 1)
    return out


def scatter_fsdp(blocks):
    size = lax.axis_size("fsdp")
    even = {
        q: blocks[q].astype(f32) + swap(blocks[q | 1].astype(bf16), "fsdp", 1).astype(f32)
        for q in range(0, size, 2)
    }
    total = even[0]
    for m in range(2, size, 2):
        total = total + swap(even[m].astype(bf16), "fsdp", m).astype(f32)
    return total


def copy_block(index_ref, from_ref, to_ref):
    to_ref[...] = from_ref[...]


def xor_blocks(values, index, count):
    rows, columns = values.shape
    width = columns // count
    return pl.pallas_call(
        copy_block,
        grid_spec=pltpu.PrefetchScalarGridSpec(
            num_scalar_prefetch=1,
            grid=(count,),
            in_specs=[pl.BlockSpec((rows, width), lambda q, at: (0, jnp.bitwise_xor(q, at[0])))],
            out_specs=pl.BlockSpec((rows, width), lambda q, at: (0, q)),
        ),
        out_shape=jax.ShapeDtypeStruct(values.shape, values.dtype),
    )(index.astype(jnp.int32).reshape(1), values)


def xor_small(values, index, count):
    rows, columns = values.shape
    blocks = jnp.arange(count, dtype=jnp.int32)
    swap_matrix = (blocks[:, None] ^ index == blocks[None, :])[None, :, :, None]
    parts = values.reshape(rows, 1, count, columns // count)
    return jnp.sum(jnp.where(swap_matrix, parts, 0.0), axis=2).reshape(rows, columns)


def body(
    inputs,
    doc_starts,
    routes,
    gate_weights,
    qkv_w,
    out_w,
    norm_gains,
    head_gains,
    gate_up,
    down_t,
    cotangent,
):
    n_ctx, n_fsdp = lax.axis_size("ctx"), lax.axis_size("fsdp")
    c, f = lax.axis_index("ctx"), lax.axis_index("fsdp")
    tok_rows, model_width = inputs.shape[1:]
    head_dim = head_gains.shape[0] * n_fsdp
    own_width = model_width // n_ctx
    own_heads = own_width // head_dim
    score_scale = head_dim ** (-0.5)
    top_count = routes.shape[2]
    hidden_units = down_t.shape[2]
    local_experts = gate_up.shape[1]
    experts_all = local_experts * n_fsdp
    capacity = tok_rows * top_count * 5 // (experts_all * 4)
    slots = n_fsdp * capacity
    stream_len = doc_starts.shape[1]
    half_dim = head_dim // 2

    x_low = inputs[0]
    x_rows = x_low.astype(f32)
    cot_low = cotangent[0]
    cot_rows = cot_low.astype(f32)

    x_all = jnp.concatenate(gather_ctx(xor_blocks(x_low, f, n_fsdp)), axis=0)
    qkv_own = lax.dynamic_slice_in_dim(qkv_w, c * own_width, own_width, axis=2)
    qkv_all = jnp.concatenate(gather_fsdp(qkv_own), axis=0)
    units = n_ctx * n_fsdp
    out_piece_rows = out_w.shape[0] // n_ctx
    flat = lambda ci, fi: ci * n_fsdp + fi
    to_heads = [(flat(u % n_ctx, u // n_ctx), flat(u // n_fsdp, u % n_fsdp)) for u in range(units)]
    out_piece = lax.ppermute(
        lax.dynamic_slice_in_dim(out_w, c * out_piece_rows, out_piece_rows, axis=0),
        ("ctx", "fsdp"),
        to_heads,
    )
    out_pieces = gather_fsdp(out_piece)
    out_own = jnp.zeros((own_width, model_width), bf16)
    for q, piece in enumerate(out_pieces):
        out_own = lax.dynamic_update_slice_in_dim(out_own, piece, (f ^ q) * out_piece_rows, axis=0)

    norm_rows, head_rows = norm_gains.shape[0], head_gains.shape[0]
    small = jnp.concatenate(
        [
            norm_gains.astype(f32).T.reshape(-1),
            routes[0].astype(f32).T.reshape(-1),
            gate_weights[0].T.reshape(-1),
            head_gains.astype(f32).T.reshape(-1),
        ]
    )
    small_rows = -(-small.shape[0] // 1024) * 8
    small = jnp.pad(small, (0, small_rows * 128 - small.shape[0])).reshape(small_rows, 128)
    small = jnp.stack(gather_fsdp(small)).reshape(n_fsdp, small_rows * 128)
    parts = jnp.split(
        small, np.cumsum([2 * norm_rows, 2 * tok_rows * top_count, 2 * head_rows]), axis=1
    )
    norm_xor = parts[0].reshape(n_fsdp, 2, norm_rows).transpose(1, 0, 2).reshape(2, model_width)
    routed = parts[1].reshape(n_fsdp, 2 * top_count, tok_rows).transpose(1, 0, 2)
    head_xor = parts[2].reshape(n_fsdp, 2, head_rows).transpose(1, 0, 2).reshape(2, head_dim)
    norm_one, norm_two = xor_small(norm_xor, f, n_fsdp)
    head_q, head_k = xor_small(head_xor, f, n_fsdp)

    cot_all = jnp.concatenate(gather_fsdp(cot_low), axis=0)
    gate_up_all = lax.all_gather(gate_up.transpose(1, 0, 2), "ctx", axis=1, tiled=True)
    down_all = lax.all_gather(down_t.transpose(1, 0, 2), "ctx", axis=1, tiled=True)

    places = jnp.arange(stream_len, dtype=jnp.int32)
    spots = ((c ^ (places // tok_rows)) * tok_rows + places % tok_rows).astype(jnp.int32)
    starts = doc_starts[0]
    reach = spots[:, None] >= places[None, :]
    doc_ids = jnp.sum(jnp.where(reach, starts[None, :], 0), axis=1)
    begins = jnp.max(jnp.where(reach & (starts[None, :] == 1), places[None, :], 0), axis=1)
    relative = spots - begins
    same_doc = (doc_ids[:, None] == doc_ids[None, :])[None]
    frequency = jnp.exp(jnp.arange(half_dim, dtype=f32) * (-2.0 / head_dim) * math.log(ROPE_BASE))
    angles = relative.astype(f32)[:, None] * frequency[None, :]
    cosine = jnp.cos(angles)[:, None, :]
    sine_part = jnp.sin(angles)[:, None, :]

    a1 = rms_scale(x_all.astype(f32), norm_xor[0]).astype(bf16)
    proj = jnp.einsum("td,djk->tjk", a1, qkv_all, preferred_element_type=f32)

    def prepare(q_flat, k_flat, q_gain, k_gain):
        q_heads = rms_scale(q_flat.reshape(stream_len, own_heads, head_dim), q_gain)
        k_heads = rms_scale(k_flat.reshape(stream_len, own_heads, head_dim), k_gain)
        return (rotate(q_heads, cosine, sine_part), rotate(k_heads, cosine, sine_part))

    (q_rot, k_rot), prepare_back = jax.vjp(prepare, proj[:, 0], proj[:, 1], head_q, head_k)
    q_low = q_rot.astype(bf16)
    k_low = k_rot.astype(bf16)
    v_low = proj[:, 2].reshape(stream_len, own_heads, head_dim).astype(bf16)
    logits = jnp.einsum("qhd,khd->hqk", q_low, k_low, preferred_element_type=f32) * score_scale
    logits = jnp.where(same_doc, logits, NEG_FILL)
    probs = jax.nn.softmax(logits, axis=-1)
    probs_low = probs.astype(bf16)
    attn_acc = jnp.einsum("hqk,khd->qhd", probs_low, v_low, preferred_element_type=f32)
    attn_low = attn_acc.reshape(stream_len, own_width).astype(bf16)
    mixed_heads = jnp.dot(attn_low, out_own, preferred_element_type=f32).astype(bf16)
    h_one = x_rows + scatter_ctx(
        [mixed_heads[q * tok_rows : (q + 1) * tok_rows] for q in range(n_ctx)]
    )
    a2_f32, norm_two_back = jax.vjp(rms_scale, h_one, norm_two)
    a2_low = a2_f32.astype(bf16)
    a2_all = jnp.concatenate(gather_fsdp(a2_low), axis=0)

    tokens = n_fsdp * tok_rows
    routed = routed.reshape(2 * top_count, tokens)
    own = (f * local_experts + jnp.arange(local_experts, dtype=jnp.int32)).astype(f32)
    chosen = routed[None, :top_count] == own[:, None, None]
    member = jnp.any(chosen, axis=1)
    weight = jnp.sum(jnp.where(chosen, routed[None, top_count:], 0.0), axis=1)
    token_ids = jnp.arange(tokens, dtype=jnp.int32)
    before = (token_ids[:, None] < token_ids[None, :]).astype(bf16)
    rank = jnp.dot(member.astype(bf16), before, preferred_element_type=f32).astype(jnp.int32)
    place = jnp.where(member, rank, -1)
    picks = place[:, None, :] == jnp.arange(slots, dtype=jnp.int32)[None, :, None]
    slot_weight = jnp.sum(jnp.where(picks, weight[:, None, :], 0.0), axis=2)
    picks = picks.astype(bf16)

    rows = jnp.einsum("est,td->esd", picks, a2_all, preferred_element_type=f32).astype(bf16)
    scale = slot_weight[:, :, None]
    dy = jnp.einsum("est,td->esd", picks, cot_all, preferred_element_type=f32)
    dy = (scale * dy).astype(bf16)
    gate_add = jnp.einsum("erd,edk->erk", rows, gate_up_all[:, :, :hidden_units], preferred_element_type=f32)
    up_add = jnp.einsum("erd,edk->erk", rows, gate_up_all[:, :, hidden_units:], preferred_element_type=f32)
    hidden_grad = jnp.einsum("erd,edf->erf", dy, down_all, preferred_element_type=f32)
    sigmoid_g = jax.nn.sigmoid(gate_add)
    activated = gate_add * sigmoid_g
    hidden_low = (activated * up_add).astype(bf16)
    gate_grad = hidden_grad * up_add * sigmoid_g * (1.0 + gate_add * (1.0 - sigmoid_g))
    pair_grad = jnp.concatenate([gate_grad, hidden_grad * activated], axis=2).astype(bf16)
    dxe = jnp.einsum("erk,edk->erd", pair_grad, gate_up_all, preferred_element_type=f32).astype(bf16)
    grads_back = jnp.einsum("est,esd->td", picks, dxe, preferred_element_type=f32)
    grads_back = grads_back.astype(bf16).reshape(n_fsdp, tok_rows, model_width)
    da2 = scatter_fsdp([grads_back[q] for q in range(n_fsdp)])
    made = jnp.einsum("erf,edf->erd", hidden_low, down_all, preferred_element_type=f32)
    made = (scale * made.astype(bf16).astype(f32)).astype(bf16)
    mixed = jnp.einsum("est,esd->td", picks, made, preferred_element_type=f32)
    mixed = mixed.astype(bf16).reshape(n_fsdp, tok_rows, model_width)
    block_out = (h_one + scatter_fsdp([mixed[q] for q in range(n_fsdp)])).astype(bf16)

    down_part = jnp.einsum("erd,erf->edf", dy, hidden_low, preferred_element_type=f32).astype(bf16)
    down_grad = lax.psum_scatter(down_part, "ctx", scatter_dimension=1, tiled=True).astype(f32)
    pair_part = jnp.einsum("erd,erk->edk", rows, pair_grad, preferred_element_type=f32).astype(bf16)
    gate_up_grad = lax.psum_scatter(pair_part, "ctx", scatter_dimension=1, tiled=True).astype(f32)

    dh_part, gain_two_grad = norm_two_back(da2)
    dh_one = cot_rows + dh_part
    dattn = jnp.concatenate(gather_ctx(dh_one.astype(bf16)), axis=0)
    d_out = jnp.einsum("tk,dk->td", dattn, out_own, preferred_element_type=f32)
    d_out = d_out.astype(bf16).reshape(stream_len, own_heads, head_dim)
    prob_grad = jnp.einsum("qhd,khd->hqk", d_out, v_low, preferred_element_type=f32)
    row_delta = jnp.sum(probs * prob_grad, axis=2, keepdims=True)
    logit_grad = (probs * (prob_grad - row_delta)).astype(bf16)
    dq = jnp.einsum("hqk,khd->qhd", logit_grad, k_low, preferred_element_type=f32) * score_scale
    dk = jnp.einsum("hqk,qhd->khd", logit_grad, q_low, preferred_element_type=f32) * score_scale
    dv = jnp.einsum("hqk,qhd->khd", probs_low, d_out, preferred_element_type=f32)
    dq_proj, dk_proj, q_gain_grad, k_gain_grad = prepare_back(
        (dq.astype(bf16).astype(f32), dk.astype(bf16).astype(f32))
    )
    proj_grad = jnp.stack([dq_proj, dk_proj, dv.reshape(stream_len, own_width)], axis=1).astype(bf16)
    da1 = jnp.einsum("tjk,djk->td", proj_grad, qkv_all, preferred_element_type=f32).astype(bf16)
    da1 = scatter_ctx([da1[q * tok_rows : (q + 1) * tok_rows] for q in range(n_ctx)])
    da1 = xor_blocks(da1, f, n_fsdp)
    _, norm_one_back = jax.vjp(rms_scale, x_rows, norm_one)
    dx_part, gain_one_grad = norm_one_back(da1)
    inputs_grad = dh_one + dx_part

    qkv_part = jnp.einsum("td,tjk->djk", a1, proj_grad, preferred_element_type=f32).astype(bf16)
    row_count = qkv_w.shape[0]
    qkv_sum = scatter_fsdp([qkv_part[q * row_count : (q + 1) * row_count] for q in range(n_fsdp)])
    out_part = jnp.einsum("td,tk->dk", attn_low, dattn, preferred_element_type=f32).astype(bf16)
    out_sum = scatter_fsdp(
        [
            lax.dynamic_slice_in_dim(out_part, (f ^ q) * out_piece_rows, out_piece_rows, axis=0)
            for q in range(n_fsdp)
        ]
    )
    qkv_grad = jnp.zeros((row_count, 3, model_width), f32)
    for q, piece in enumerate(gather_ctx(qkv_sum.astype(bf16))):
        qkv_grad = lax.dynamic_update_slice_in_dim(
            qkv_grad, piece.astype(f32), (c ^ q) * own_width, axis=2
        )
    out_sum = lax.ppermute(out_sum.astype(bf16), ("ctx", "fsdp"), [(b, a) for a, b in to_heads])
    out_grad = jnp.zeros((row_count, model_width), f32)
    for q, piece in enumerate(gather_ctx(out_sum)):
        out_grad = lax.dynamic_update_slice_in_dim(
            out_grad, piece.astype(f32), (c ^ q) * out_piece_rows, axis=0
        )

    gain_sums = jnp.concatenate(
        [jnp.stack([gain_one_grad, gain_two_grad]), jnp.stack([q_gain_grad, k_gain_grad])], axis=1
    )
    for axis in ("fsdp", "ctx"):
        for bit in bits_down(lax.axis_size(axis)):
            gain_sums = gain_sums + swap(gain_sums, axis, bit)
    norm_grad = lax.dynamic_slice_in_dim(gain_sums, f * norm_rows, norm_rows, axis=1).T
    head_grad = lax.dynamic_slice_in_dim(
        gain_sums, model_width + f * head_rows, head_rows, axis=1
    ).T
    return (
        block_out[None],
        inputs_grad[None],
        qkv_grad,
        out_grad,
        norm_grad,
        head_grad,
        gate_up_grad.transpose(1, 0, 2),
        down_grad.transpose(1, 0, 2),
    )


def solution(mesh):
    return jax.shard_map(
        body,
        mesh=mesh,
        in_specs=(
            P("fsdp", "ctx", None),
            P("fsdp", None),
            P("fsdp", "ctx", None),
            P("fsdp", "ctx", None),
            P("fsdp", None, None),
            P("fsdp", None),
            P("fsdp", None),
            P("fsdp", None),
            P("ctx", "fsdp", None),
            P("ctx", "fsdp", None),
            P("fsdp", "ctx", None),
        ),
        out_specs=(
            P("fsdp", "ctx", None),
            P("fsdp", "ctx", None),
            P("fsdp", None, None),
            P("fsdp", None),
            P("fsdp", None),
            P("fsdp", None),
            P("ctx", "fsdp", None),
            P("ctx", "fsdp", None),
        ),
        check_vma=False,
    )
```

```python
import functools
import math

import jax
import jax.numpy as jnp
from jax import lax
from jax.experimental import pallas as pl
from jax.experimental.pallas import tpu as pltpu
from jax.sharding import PartitionSpec as P

EPS = 1e-06
ROPE_BASE = 10000.0
NEG_FILL = -1e30
LANES = 128
f32 = jnp.float32
bf16 = jnp.bfloat16
VMEM = pl.BlockSpec(memory_space=pltpu.VMEM)
SMEM = pl.BlockSpec(memory_space=pltpu.SMEM)
NN = (((1,), (0,)), ((), ()))
NT = (((1,), (1,)), ((), ()))
TN = (((0,), (0,)), ((), ()))


def mm(a, b, dims=NN):
    return lax.dot_general(a, b, dims, preferred_element_type=f32)


def rms_scale(values, gain):
    return values * lax.rsqrt(jnp.mean(values * values, axis=-1, keepdims=True) + EPS) * gain


def cost(microseconds):
    return pl.CostEstimate(flops=int(microseconds * 1e9), bytes_accessed=0, transcendentals=0)


def params(mib):
    return pltpu.CompilerParams(vmem_limit_bytes=mib * 2**20)


def after(value, *others):
    return lax.optimization_barrier((value, *others))[0]


def swap(value, axis, mask):
    size = lax.axis_size(axis)
    return lax.ppermute(value, axis, [(i, i ^ mask) for i in range(size)])


def bits_down(size):
    return [1 << b for b in reversed(range(size.bit_length() - 1))]


def gather_ctx(block):
    pieces = {0: block}
    for bit in bits_down(lax.axis_size("ctx")):
        pieces.update({q | bit: swap(piece, "ctx", bit) for q, piece in list(pieces.items())})
    return [pieces[q] for q in range(len(pieces))]


def folded_order(size):
    order = [0]
    for bit in bits_down(size):
        order = order + [q | bit for q in order]
    return order


def scatter_ctx(blocks):
    size = lax.axis_size("ctx")
    for bit in reversed(bits_down(size)):
        half = blocks.shape[0] // 2
        got = swap(blocks[half:], "ctx", bit)
        blocks = blocks[:half].astype(f32) + got.astype(f32)
        if half > 1:
            blocks = blocks.astype(bf16)
    return blocks[0]


def far_masks():
    return list(range(2, lax.axis_size("fsdp"), 2))


def gather_far(block):
    size = lax.axis_size("fsdp")
    masks = sorted(range(2, size, 2), key=lambda m: (m == size - 2, m == 2))
    far = {m: swap(block, "fsdp", m) for m in masks}
    return [block] + [far[m] for m in range(2, size, 2)]


def gather_near(pieces):
    out = []
    for piece in pieces:
        out += [piece, swap(piece, "fsdp", 1)]
    return out


def gather_fsdp(block):
    return gather_near(gather_far(block))


def scatter_first(even_a, odd_a, pairs_b):
    got = swap(odd_a, "fsdp", 1)
    sums_a = [even_a[i].astype(f32) + got[i].astype(f32) for i in range(even_a.shape[0])]
    sums_a = [sums_a[0]] + [part.astype(bf16) for part in sums_a[1:]]
    sum_b = pairs_b[0].astype(f32)
    for i, m in enumerate(far_masks()):
        sum_b = sum_b + swap(pairs_b[i + 1], "fsdp", m).astype(f32)
    return sums_a, sum_b[0], sum_b[1].astype(bf16)


def scatter_second(first, *others):
    sums_a, own_b, other_b = first
    total_a = sums_a[0]
    for i, m in enumerate(far_masks()):
        total_a = total_a + swap(after(sums_a[i + 1], *others), "fsdp", m).astype(f32)
    return total_a, own_b + swap(after(other_b, *others), "fsdp", 1).astype(f32)


def split_blocks(blocks, size):
    pairs = blocks.reshape(blocks.shape[0] // 2, 2, *blocks.shape[1:])
    parts_b = [pairs[i, :, :, size:] for i in range(pairs.shape[0])]
    return pairs[:, 0, :, :size], pairs[:, 1, :, :size], parts_b


def lane_chunk(values, flat):
    width = values.shape[1]
    row, lane = flat // width, flat % width
    return values[row : row + 1, lane : lane + LANES]


def at_block(block, width):
    return pl.ds(pl.multiple_of(block * width, LANES), width)


def rope(values, cosine, sine):
    return values * cosine + pltpu.roll(values, values.shape[1] // 2, 1) * sine


def rope_back(grads, cosine, sine):
    return grads * cosine + pltpu.roll(grads * sine, grads.shape[1] // 2, 1)


def over_blocks(block, carry, length, size):
    if length == size:
        return block(slice(0, size), carry)
    step = lambda i, kept: block(pl.ds(pl.multiple_of(i * size, size), size), kept)
    return lax.fori_loop(0, length // size, step, carry)


def out_kernel(f_ref, attn_ref, *refs):
    piece_refs, (own_ref, mixed_ref) = refs[:-2], refs[-2:]
    rows = piece_refs[0].shape[0]
    for q, piece_ref in enumerate(piece_refs):
        spot = pl.ds(pl.multiple_of(jnp.bitwise_xor(f_ref[0], q) * rows, rows), rows)
        own_ref[spot, :] = piece_ref[...]
    mixed_ref[...] = mm(attn_ref[...], own_ref[...]).astype(bf16)


def attend_kernel(sizes, f_ref, *refs):
    n_ctx, n_fsdp, head_dim, head_rows, norm_rows, q_rows = sizes
    x_refs, refs = refs[:n_ctx], refs[n_ctx:]
    w_refs, refs = refs[:n_fsdp], refs[n_fsdp:]
    cos_ref, sin_ref, dq_ref, dk_ref = refs[:4]
    a1_ref, qp_ref, kp_ref, q_ref, k_ref, v_ref, o_ref, gains_ref, heads_ref = refs[4:]
    f = f_ref[0]
    tok = x_refs[0].shape[0]
    length, width = q_ref.shape
    lane = lax.broadcasted_iota(jnp.int32, (8, LANES), 1)
    heads = [jnp.zeros((8, LANES), f32), jnp.zeros((8, LANES), f32)]
    for q in range(n_fsdp):
        block = jnp.bitwise_xor(f, q)
        extra = w_refs[q][3 * norm_rows :, :].astype(f32)
        for row in range(2):
            for k in range(norm_rows // LANES):
                spot = pl.ds(pl.multiple_of(block * norm_rows + k * LANES, LANES), LANES)
                gains_ref[row : row + 1, spot] = lane_chunk(extra, row * norm_rows + k * LANES)
            piece = jnp.broadcast_to(lane_chunk(extra, 2 * norm_rows + row * LANES), (8, LANES))
            piece = pltpu.roll(piece, block * head_rows, 1)
            heads[row] = jnp.where(lane // head_rows == block, piece, heads[row])
    for row in range(2):
        heads_ref[row : row + 1, :] = heads[row][:1]
    for i, x_ref in enumerate(x_refs):
        x = x_ref[...].astype(f32)
        a1_ref[i * tok : (i + 1) * tok, :] = rms_scale(x, gains_ref[0:1, :]).astype(bf16)
    outs = []
    for j in range(3):
        acc = None
        for q in range(n_fsdp):
            part = mm(
                a1_ref[:, at_block(jnp.bitwise_xor(f, q), norm_rows)],
                w_refs[q][j * norm_rows : (j + 1) * norm_rows, :],
            )
            acc = part if acc is None else acc + part
        if j == 0:
            qp_ref[...] = acc
        elif j == 1:
            kp_ref[...] = acc
        else:
            v_ref[...] = acc.astype(bf16)
    cosine, sine = cos_ref[...], sin_ref[...]
    for h in range(width // head_dim):
        cols = slice(h * head_dim, (h + 1) * head_dim)
        for from_ref, to_ref, row in ((qp_ref, q_ref, 0), (kp_ref, k_ref, 1)):
            normed = rms_scale(from_ref[:, cols], heads_ref[row : row + 1, :])
            to_ref[:, cols] = rope(normed, cosine, sine).astype(bf16)

        def block(rows, _):
            logits = mm(q_ref[rows, cols], k_ref[:, cols], NT) * head_dim**-0.5
            logits = jnp.where(dq_ref[rows, :] == dk_ref[...], logits, NEG_FILL)
            weights = jnp.exp(logits - jnp.max(logits, axis=1, keepdims=True))
            probs = weights * (1.0 / jnp.sum(weights, axis=1, keepdims=True))
            o_ref[rows, cols] = mm(probs.astype(bf16), v_ref[:, cols]).astype(bf16)
            return 0

        over_blocks(block, 0, length, q_rows)


def attend_back_kernel(sizes, *refs):
    n_ctx, head_dim, q_rows = sizes
    g_refs, refs = refs[:n_ctx], refs[n_ctx:]
    out_ref, q_ref, k_ref, v_ref, qp_ref, kp_ref, cos_ref, sin_ref, dq_ref, dk_ref, heads_ref = refs[:11]
    d_ref, hg_ref, go_ref = refs[11:]
    tok = g_refs[0].shape[0]
    length, width = q_ref.shape
    scale = head_dim**-0.5
    for i, g_ref in enumerate(g_refs):
        go_ref[i * tok : (i + 1) * tok, :] = mm(g_ref[...], out_ref[...], NT).astype(bf16)
    cosine, sine = cos_ref[...], sin_ref[...]
    sums = [None, None]
    for h in range(width // head_dim):
        cols = slice(h * head_dim, (h + 1) * head_dim)
        key, value = k_ref[:, cols], v_ref[:, cols]

        def block(rows, sums_of):
            d_key, d_value = sums_of
            query, d_out = q_ref[rows, cols], go_ref[rows, cols]
            logits = mm(query, key, NT) * scale
            logits = jnp.where(dq_ref[rows, :] == dk_ref[...], logits, NEG_FILL)
            weights = jnp.exp(logits - jnp.max(logits, axis=1, keepdims=True))
            probs = weights * (1.0 / jnp.sum(weights, axis=1, keepdims=True))
            d_prob = mm(d_out, value, NT)
            delta = jnp.sum(probs * d_prob, axis=1, keepdims=True)
            d_logit = (probs * (d_prob - delta)).astype(bf16)
            d_ref[0, rows, cols] = (mm(d_logit, key) * scale).astype(bf16)
            return (
                d_key + mm(d_logit, query, TN),
                d_value + mm(probs.astype(bf16), d_out, TN),
            )

        zeros = jnp.zeros((length, head_dim), f32)
        d_key, d_value = over_blocks(block, (zeros, zeros), length, q_rows)
        d_query = d_ref[0, :, cols].astype(f32)
        d_ref[2, :, cols] = d_value.astype(bf16)
        for row, grads, proj_ref in ((0, d_query, qp_ref), (1, d_key * scale, kp_ref)):
            grads = rope_back(grads.astype(bf16).astype(f32), cosine, sine)
            values = proj_ref[:, cols]
            root = lax.rsqrt(jnp.mean(values * values, axis=1, keepdims=True) + EPS)
            normed = values * root
            part = jnp.sum(grads * normed, axis=0, keepdims=True)
            sums[row] = part if sums[row] is None else sums[row] + part
            grads = grads * heads_ref[row : row + 1, :]
            inner = jnp.mean(grads * normed, axis=1, keepdims=True)
            d_ref[row, :, cols] = (root * (grads - normed * inner)).astype(bf16)
    for row in range(2):
        hg_ref[row : row + 1, :] = sums[row]


def project_back_kernel(sizes, f_ref, *refs):
    n_ctx, n_fsdp, head_rows, norm_rows = sizes
    x_refs, refs = refs[:n_ctx], refs[n_ctx:]
    w_refs, refs = refs[:n_fsdp], refs[n_fsdp:]
    a1_ref, d_ref, hg_ref, gain_two_ref = refs[:4]
    pay_refs, (da_ref, root_ref, extra_ref) = refs[4:-3], refs[-3:]
    pay_a, pay_b = pay_refs[:2], pay_refs[2:]
    f = f_ref[0]
    tok = x_refs[0].shape[0]
    width = d_ref.shape[2]
    for i, x_ref in enumerate(x_refs):
        x = x_ref[...].astype(f32)
        root_ref[i * tok : (i + 1) * tok, :] = lax.rsqrt(jnp.mean(x * x, axis=1, keepdims=True) + EPS)
    for q in range(n_fsdp):
        block = jnp.bitwise_xor(f, q)
        spot = at_block(block, norm_rows)
        flipped = a1_ref[:, spot].astype(f32).T.astype(bf16)
        da = None
        for j in range(3):
            rows = slice(j * norm_rows, (j + 1) * norm_rows)
            part = mm(d_ref[j], w_refs[q][rows, :], NT)
            da = part if da is None else da + part
            grad = mm(flipped, d_ref[j]).astype(bf16)
            if j == 2:
                pay_b[q // 2][q % 2, :norm_rows, :] = grad
            else:
                pay_a[q % 2][q // 2, rows, :] = grad
        da_ref[:, spot] = da.astype(bf16)
        gain = None
        for i, x_ref in enumerate(x_refs):
            rows = slice(i * tok, (i + 1) * tok)
            part = x_ref[:, spot].astype(f32) * root_ref[rows, :] * da[rows]
            part = jnp.sum(part, axis=0, keepdims=True)
            gain = part if gain is None else gain + part
        extra_ref[...] = jnp.zeros(extra_ref.shape, f32)
        for k in range(norm_rows // LANES):
            lanes = slice(k * LANES, (k + 1) * LANES)
            row, lane = k * LANES // width, k * LANES % width
            extra_ref[row : row + 1, lane : lane + LANES] = gain[:, lanes]
            two = norm_rows + k * LANES
            row, lane = two // width, two % width
            spot_two = pl.ds(pl.multiple_of(block * norm_rows + k * LANES, LANES), LANES)
            extra_ref[row : row + 1, lane : lane + LANES] = gain_two_ref[0:1, spot_two]
        for r in range(2):
            flat = 2 * norm_rows + r * LANES
            row, lane = flat // width, flat % width
            turned = jnp.broadcast_to(hg_ref[r : r + 1, :], (8, LANES))
            turned = pltpu.roll(turned, (n_fsdp - block) * head_rows, 1)
            extra_ref[row : row + 1, lane : lane + LANES] = turned[:1]
        pay_b[q // 2][q % 2, norm_rows:, :] = extra_ref[...].astype(bf16)


def finish_kernel(sizes, c_ref, *refs):
    n_ctx, norm_rows = sizes
    pay_refs, out_refs = refs[:n_ctx], refs[n_ctx : 2 * n_ctx]
    qkv_ref, out_ref = refs[2 * n_ctx :]
    c = c_ref[0]
    width = pay_refs[0].shape[1]
    piece_rows = out_refs[0].shape[0]
    for q in range(n_ctx):
        block = jnp.bitwise_xor(c, q)
        for j in range(3):
            rows = slice(j * norm_rows, (j + 1) * norm_rows)
            qkv_ref[j, :, at_block(block, width)] = pay_refs[q][rows, :].astype(f32)
        spot = pl.ds(pl.multiple_of(block * piece_rows, piece_rows), piece_rows)
        out_ref[spot, :] = out_refs[q][...].astype(f32)


def dispatch_kernel(picks_ref, scale_ref, *refs):
    piece_refs, dy_ref, all_ref = refs[:-2], refs[-2], refs[-1]
    tok = piece_refs[0].shape[0]

    @pl.when(pl.program_id(0) == 0)
    def _():
        for q, piece_ref in enumerate(piece_refs):
            all_ref[q * tok : (q + 1) * tok, :] = piece_ref[...]

    dy_ref[0] = (mm(picks_ref[0], all_ref[...]) * scale_ref[0]).astype(bf16)


def hidden_kernel(picks_ref, dy_ref, wg_ref, wu_ref, wd_ref, *refs):
    piece_refs, (rows_ref, hid_ref, dg_ref, du_ref, all_ref) = refs[:-5], refs[-5:]
    tok = piece_refs[0].shape[0]
    first = pl.program_id(1) == 0

    @pl.when(first & (pl.program_id(0) == 0))
    def _():
        for q, piece_ref in enumerate(piece_refs):
            all_ref[q * tok : (q + 1) * tok, :] = piece_ref[...]

    @pl.when(first)
    def _():
        rows_ref[0] = mm(picks_ref[0], all_ref[...]).astype(bf16)

    rows = rows_ref[0]
    gate = mm(rows, wg_ref[0])
    up = mm(rows, wu_ref[0])
    d_hid = mm(dy_ref[0], wd_ref[0])
    sig = 1.0 / (1.0 + jnp.exp(-gate))
    act = gate * sig
    hid_ref[0] = (act * up).astype(bf16)
    dg_ref[0] = (d_hid * up * sig * (1.0 + gate * (1.0 - sig))).astype(bf16)
    du_ref[0] = (d_hid * act).astype(bf16)


def body(
    inputs,
    doc_starts,
    routes,
    gate_weights,
    qkv_w,
    out_w,
    norm_gains,
    head_gains,
    gate_up,
    down_t,
    cotangent,
):
    n_ctx, n_fsdp = lax.axis_size("ctx"), lax.axis_size("fsdp")
    c, f = lax.axis_index("ctx"), lax.axis_index("fsdp")
    c_at, f_at = c.astype(jnp.int32).reshape(1), f.astype(jnp.int32).reshape(1)
    tok_rows, model_width = inputs.shape[1:]
    norm_rows, head_rows = norm_gains.shape[0], head_gains.shape[0]
    head_dim = head_rows * n_fsdp
    own_width = model_width // n_ctx
    top_count = routes.shape[2]
    hidden_units = down_t.shape[2]
    local_experts = gate_up.shape[1]
    experts_all = local_experts * n_fsdp
    capacity = tok_rows * top_count * 5 // (experts_all * 4)
    slots = -(-n_fsdp * capacity // 16) * 16
    stream_len = doc_starts.shape[1]
    q_rows = min(512, stream_len)
    half_dim = head_dim // 2
    tokens = n_fsdp * tok_rows
    order = folded_order(n_ctx)

    x_low = inputs[0]
    x_rows = x_low.astype(f32)
    cot_low = cotangent[0]
    cot_rows = cot_low.astype(f32)

    weights = gate_weights[0].T.reshape(-1)
    high = lax.reduce_precision(weights, 8, 7)
    middle = lax.reduce_precision(weights - high, 8, 7)
    gap = jnp.zeros((LANES - head_rows,), bf16)
    small = jnp.concatenate(
        [
            norm_gains.T.reshape(-1),
            head_gains[:, 0],
            gap,
            head_gains[:, 1],
            gap,
            routes[0].T.reshape(-1).astype(bf16),
            high.astype(bf16),
            middle.astype(bf16),
            (weights - high - middle).astype(bf16),
        ]
    )
    extra_rows = -(-small.shape[0] // (16 * own_width)) * 16
    small = jnp.pad(small, (0, extra_rows * own_width - small.shape[0]))
    qkv_own = lax.dynamic_slice_in_dim(qkv_w, c * own_width, own_width, axis=2)
    qkv_own = qkv_own.transpose(1, 0, 2).reshape(3 * norm_rows, own_width)
    qkv_own = jnp.concatenate([qkv_own, small.reshape(extra_rows, own_width)], axis=0)
    qkv_pieces = gather_fsdp(qkv_own)

    x_pieces = gather_ctx(x_low)
    x_pieces = [x_pieces[q] for q in order]

    units = n_ctx * n_fsdp
    out_rows = out_w.shape[0] // n_ctx
    flat = lambda ci, fi: ci * n_fsdp + fi
    to_heads = [(flat(u % n_ctx, u // n_ctx), flat(u // n_fsdp, u % n_fsdp)) for u in range(units)]
    out_piece = lax.dynamic_slice_in_dim(out_w, c * out_rows, out_rows, axis=0)
    out_piece = lax.ppermute(after(out_piece, *x_pieces), ("ctx", "fsdp"), to_heads)
    split = model_width * 11 // (16 * LANES) * LANES
    out_far = gather_far(after(out_piece, qkv_pieces[-1]))
    out_pieces = gather_near(out_far)

    cot_far = gather_far(after(cot_low, *out_far))
    gate_up_all = lax.all_gather(gate_up.transpose(1, 0, 2), "ctx", axis=1, tiled=True)
    down_all = lax.all_gather(
        down_t.transpose(1, 0, 2), "ctx", axis=1, tiled=True
    )

    places = jnp.arange(stream_len, dtype=jnp.int32)
    blocks = jnp.repeat(jnp.asarray(order, jnp.int32), tok_rows)
    spots = (c ^ blocks) * tok_rows + places % tok_rows
    starts = doc_starts[0]
    reach = spots[:, None] >= places[None, :]
    doc_ids = jnp.sum(jnp.where(reach, starts[None, :], 0), axis=1)
    begins = jnp.max(jnp.where(reach & (starts[None, :] == 1), places[None, :], 0), axis=1)
    relative = spots - begins
    frequency = jnp.exp(jnp.arange(half_dim, dtype=f32) * (-2.0 / head_dim) * math.log(ROPE_BASE))
    angles = relative.astype(f32)[:, None] * frequency[None, :]
    cosine = jnp.cos(angles)
    cosine = jnp.concatenate([cosine, cosine], axis=1)
    sine = jnp.sin(angles)
    sine = jnp.concatenate([-sine, sine], axis=1)
    doc_q, doc_k = doc_ids[:, None], doc_ids[None, :]

    act = jax.ShapeDtypeStruct((stream_len, own_width), bf16)
    wide = jax.ShapeDtypeStruct((stream_len, own_width), f32)
    a1, q_proj, k_proj, q_low, k_low, v_low, attn_low, gains, heads = pl.pallas_call(
        functools.partial(
            attend_kernel, (n_ctx, n_fsdp, head_dim, head_rows, norm_rows, q_rows)
        ),
        in_specs=[SMEM] + [VMEM] * (n_ctx + n_fsdp + 4),
        out_specs=[VMEM] * 9,
        out_shape=[
            jax.ShapeDtypeStruct((stream_len, model_width), bf16),
            wide,
            wide,
            act,
            act,
            act,
            act,
            jax.ShapeDtypeStruct((2, model_width), f32),
            jax.ShapeDtypeStruct((2, head_dim), f32),
        ],
        compiler_params=params(48),
        cost_estimate=cost(1),
        name="attend",
    )(f_at, *x_pieces, *qkv_pieces, cosine, sine, doc_q, doc_k)
    out_own, mixed_heads = pl.pallas_call(
        out_kernel,
        in_specs=[SMEM] + [VMEM] * (n_fsdp + 1),
        out_specs=[VMEM] * 2,
        out_shape=[
            jax.ShapeDtypeStruct((own_width, model_width), bf16),
            jax.ShapeDtypeStruct((stream_len, model_width), bf16),
        ],
        compiler_params=params(40),
        cost_estimate=cost(1),
        name="out",
    )(f_at, attn_low, *out_pieces)
    h_one = x_rows + scatter_ctx(mixed_heads.reshape(n_ctx, tok_rows, model_width))
    a2_f32, norm_two_back = jax.vjp(rms_scale, h_one, gains[1])
    a2_low = a2_f32.astype(bf16)
    a2_pieces = gather_fsdp(a2_low)
    cot_pieces = gather_near([after(piece, a2_low) for piece in cot_far])

    extras = jnp.stack([piece[3 * norm_rows :].reshape(-1) for piece in qkv_pieces]).astype(f32)
    route_at = 2 * norm_rows + 2 * LANES
    count = tok_rows * top_count
    spread = extras[:, route_at : route_at + 4 * count].reshape(n_fsdp, 4, top_count, tok_rows)
    spread = spread.transpose(1, 2, 0, 3).reshape(4, top_count, tokens)
    own = (f * local_experts + jnp.arange(local_experts, dtype=jnp.int32)).astype(f32)
    chosen = spread[0][None] == own[:, None, None]
    token_weight = spread[1] + spread[2] + spread[3]
    member = jnp.any(chosen, axis=1)
    weight = jnp.sum(jnp.where(chosen, token_weight[None], 0.0), axis=1)
    token_ids = jnp.arange(tokens, dtype=jnp.int32)
    before = (token_ids[:, None] < token_ids[None, :]).astype(bf16)
    rank = mm(member.astype(bf16), before).astype(jnp.int32)
    place = jnp.where(member, rank, -1)
    slot_ids = jnp.arange(slots, dtype=jnp.int32)
    picks = place[:, None, :] == slot_ids[None, :, None]
    scale = jnp.sum(jnp.where(picks, weight[:, None, :], 0.0), axis=2, keepdims=True)
    picks = picks.astype(bf16)
    tile = 512
    per_expert = lambda *shape: pl.BlockSpec((1,) + shape, lambda e, j: (e, 0, 0))
    whole = lambda *shape: pl.BlockSpec(shape, lambda *_: (0,) * len(shape))
    column = lambda rows_of, shift: pl.BlockSpec((1, rows_of, tile), lambda e, j: (e, 0, j + shift))
    piece_specs = [whole(tok_rows, model_width)] * n_fsdp
    row_shape = jax.ShapeDtypeStruct((local_experts, slots, model_width), bf16)
    gathered = [pltpu.VMEM((tokens, model_width), bf16)]
    dy = pl.pallas_call(
        dispatch_kernel,
        grid=(local_experts,),
        in_specs=[
            pl.BlockSpec((1, slots, tokens), lambda e: (e, 0, 0)),
            pl.BlockSpec((1, slots, 1), lambda e: (e, 0, 0)),
        ]
        + piece_specs,
        out_specs=pl.BlockSpec((1, slots, model_width), lambda e: (e, 0, 0)),
        out_shape=row_shape,
        scratch_shapes=gathered,
        compiler_params=params(40),
        cost_estimate=cost(5),
        name="dispatch",
    )(picks, scale, *cot_pieces)
    hid_shape = jax.ShapeDtypeStruct((local_experts, slots, hidden_units), bf16)
    rows, hidden_low, gate_grad, up_grad = pl.pallas_call(
        hidden_kernel,
        grid=(local_experts, hidden_units // tile),
        in_specs=[
            per_expert(slots, tokens),
            per_expert(slots, model_width),
            column(model_width, 0),
            column(model_width, hidden_units // tile),
            column(model_width, 0),
        ]
        + piece_specs,
        out_specs=[per_expert(slots, model_width)] + [column(slots, 0)] * 3,
        out_shape=[
            row_shape,
            hid_shape,
            hid_shape,
            hid_shape,
        ],
        scratch_shapes=gathered,
        compiler_params=params(48),
        cost_estimate=cost(20),
        name="hidden",
    )(picks, dy, gate_up_all, gate_up_all, down_all, *a2_pieces)

    pair_grad = jnp.concatenate([gate_grad, up_grad], axis=2)

    token_blocks = lambda values: split_blocks(values.reshape(n_fsdp, tok_rows, model_width), split)
    dxe = jnp.einsum("erk,edk->erd", pair_grad, gate_up_all, preferred_element_type=f32).astype(bf16)
    grads_back = jnp.einsum("est,esd->td", picks, dxe, preferred_element_type=f32).astype(bf16)
    dx_first = scatter_first(*token_blocks(grads_back))
    down_part = jnp.einsum(
        "erd,erf->edf", after(dy, grads_back), hidden_low, preferred_element_type=f32
    ).astype(bf16)
    down_grad = lax.psum_scatter(down_part, "ctx", scatter_dimension=1, tiled=True).astype(f32)
    pair_part = jnp.einsum(
        "erd,erk->edk", after(rows, grads_back), pair_grad, preferred_element_type=f32
    ).astype(bf16)
    gate_up_grad = lax.psum_scatter(pair_part, "ctx", scatter_dimension=1, tiled=True).astype(f32)
    da2 = jnp.concatenate(scatter_second(dx_first, pair_part), axis=1)
    made = jnp.einsum(
        "erf,edf->erd", after(hidden_low, grads_back), down_all, preferred_element_type=f32
    )
    made = (scale * made.astype(bf16).astype(f32)).astype(bf16)
    mixed = jnp.einsum("est,esd->td", picks, made, preferred_element_type=f32).astype(bf16)
    mixed_first = scatter_first(*token_blocks(mixed))

    dh_part, gain_two_grad = norm_two_back(da2)
    dh_one = cot_rows + dh_part
    dattn_pieces = gather_ctx(dh_one.astype(bf16))
    dattn_pieces = [dattn_pieces[q] for q in order]
    proj_grad, head_grads = pl.pallas_call(
        functools.partial(attend_back_kernel, (n_ctx, head_dim, q_rows)),
        in_specs=[VMEM] * (n_ctx + 11),
        out_specs=[VMEM] * 2,
        out_shape=[
            jax.ShapeDtypeStruct((3, stream_len, own_width), bf16),
            jax.ShapeDtypeStruct((2, head_dim), f32),
        ],
        scratch_shapes=[pltpu.VMEM((stream_len, own_width), bf16)],
        compiler_params=params(56),
        cost_estimate=cost(500),
        name="attend_back",
    )(*dattn_pieces, out_own, after(q_low, *mixed_first[0], *mixed_first[1:]), k_low, v_low, q_proj, k_proj, cosine, sine, doc_q, doc_k, heads)
    dattn = jnp.concatenate(dattn_pieces, axis=0)
    out_part = mm(attn_low, dattn, TN).astype(bf16)
    out_blocks = jnp.stack(
        [
            lax.dynamic_slice_in_dim(out_part, (f ^ q) * out_rows, out_rows, axis=0)
            for q in range(n_fsdp)
        ]
    )
    out_first_sums = scatter_first(*split_blocks(out_blocks, split))
    out_parts = scatter_second(out_first_sums, proj_grad)
    out_sum = jnp.concatenate(out_parts, axis=1)
    half_stack = jax.ShapeDtypeStruct((n_fsdp // 2, 2 * norm_rows, own_width), bf16)
    pair_shape = jax.ShapeDtypeStruct((2, norm_rows + extra_rows, own_width), bf16)
    even_a, odd_a, *pairs_b, da1 = pl.pallas_call(
        functools.partial(project_back_kernel, (n_ctx, n_fsdp, head_rows, norm_rows)),
        in_specs=[SMEM] + [VMEM] * (n_ctx + n_fsdp + 4),
        out_specs=[VMEM] * (n_fsdp // 2 + 3),
        out_shape=[half_stack] * 2
        + [pair_shape] * (n_fsdp // 2)
        + [jax.ShapeDtypeStruct((stream_len, model_width), bf16)],
        scratch_shapes=[
            pltpu.VMEM((stream_len, 1), f32),
            pltpu.VMEM((extra_rows, own_width), f32),
        ],
        compiler_params=params(56),
        cost_estimate=cost(500),
        name="project_back",
    )(f_at, *x_pieces, *qkv_pieces, a1, after(proj_grad, *out_first_sums[0], out_first_sums[2]), head_grads, gain_two_grad[None])
    payload_first = scatter_first(even_a, odd_a, pairs_b)
    da1 = scatter_ctx(da1.reshape(n_ctx, tok_rows, model_width))
    out_sum = lax.ppermute(out_sum.astype(bf16), ("ctx", "fsdp"), [(b, a) for a, b in to_heads])
    out_ends = gather_ctx(out_sum)
    payload_parts = scatter_second(payload_first, *out_parts, da1, down_grad)
    qkv_sum = jnp.concatenate(payload_parts, axis=0)
    _, norm_one_back = jax.vjp(lambda x: rms_scale(x, gains[0]), x_rows)
    inputs_grad = dh_one + norm_one_back(da1)[0]
    mixed_parts = scatter_second(mixed_first, *payload_parts)
    ends = gather_ctx(qkv_sum.astype(bf16))
    qkv_grad, out_grad = pl.pallas_call(
        functools.partial(finish_kernel, (n_ctx, norm_rows)),
        in_specs=[SMEM] + [VMEM] * (2 * n_ctx),
        out_specs=[VMEM] * 2,
        out_shape=[
            jax.ShapeDtypeStruct((3, norm_rows, model_width), f32),
            jax.ShapeDtypeStruct((norm_rows, model_width), f32),
        ],
        compiler_params=params(40),
        cost_estimate=cost(1),
        name="finish",
    )(c_at, *ends, *out_ends)
    gate_up_grad = after(gate_up_grad, out_grad)
    h_one = after(h_one, out_grad, gate_up_grad)
    block_out = (h_one + jnp.concatenate(mixed_parts, axis=1)).astype(bf16)
    extras = sum(piece[3 * norm_rows :].astype(f32) for piece in ends).reshape(-1)
    norm_grad = extras[: 2 * norm_rows].reshape(2, norm_rows).T
    head_grad = extras[2 * norm_rows : route_at].reshape(2, LANES)[:, :head_rows].T
    return (
        block_out[None],
        inputs_grad[None],
        qkv_grad.transpose(1, 0, 2),
        out_grad,
        norm_grad,
        head_grad,
        gate_up_grad.transpose(1, 0, 2),
        down_grad.transpose(1, 0, 2),
    )


def solution(mesh):
    return jax.shard_map(
        body,
        mesh=mesh,
        in_specs=(
            P("fsdp", "ctx", None),
            P("fsdp", None),
            P("fsdp", "ctx", None),
            P("fsdp", "ctx", None),
            P("fsdp", None, None),
            P("fsdp", None),
            P("fsdp", None),
            P("fsdp", None),
            P("ctx", "fsdp", None),
            P("ctx", "fsdp", None),
            P("fsdp", "ctx", None),
        ),
        out_specs=(
            P("fsdp", "ctx", None),
            P("fsdp", "ctx", None),
            P("fsdp", None, None),
            P("fsdp", None),
            P("fsdp", None),
            P("fsdp", None),
            P("ctx", "fsdp", None),
            P("ctx", "fsdp", None),
        ),
        check_vma=False,
    )
```

```python
import functools
import math

import jax
import jax.numpy as jnp
from jax import lax
from jax.experimental import pallas as pl
from jax.experimental.pallas import tpu as pltpu
from jax.sharding import PartitionSpec as P

EPS = 1e-06
ROPE_BASE = 10000.0
NEG_FILL = -1e30
LANES = 128
f32 = jnp.float32
bf16 = jnp.bfloat16
VMEM = pl.BlockSpec(memory_space=pltpu.VMEM)
SMEM = pl.BlockSpec(memory_space=pltpu.SMEM)
NN = (((1,), (0,)), ((), ()))
NT = (((1,), (1,)), ((), ()))
TN = (((0,), (0,)), ((), ()))


def mm(a, b, dims=NN):
    return lax.dot_general(a, b, dims, preferred_element_type=f32)


def rms_scale(values, gain):
    return values * lax.rsqrt(jnp.mean(values * values, axis=-1, keepdims=True) + EPS) * gain


def cost(microseconds):
    return pl.CostEstimate(flops=int(microseconds * 1e9), bytes_accessed=0, transcendentals=0)


def params(mib):
    return pltpu.CompilerParams(vmem_limit_bytes=mib * 2**20)


def after(value, *others):
    return lax.optimization_barrier((value, *others))[0]


def swap(value, axis, mask):
    size = lax.axis_size(axis)
    return lax.ppermute(value, axis, [(i, i ^ mask) for i in range(size)])


def bits_down(size):
    return [1 << b for b in reversed(range(size.bit_length() - 1))]


def gather_ctx(block):
    pieces = {0: block}
    for bit in bits_down(lax.axis_size("ctx")):
        pieces.update({q | bit: swap(piece, "ctx", bit) for q, piece in list(pieces.items())})
    return [pieces[q] for q in range(len(pieces))]


def folded_order(size):
    order = [0]
    for bit in bits_down(size):
        order = order + [q | bit for q in order]
    return order


def scatter_ctx(blocks):
    size = lax.axis_size("ctx")
    for bit in reversed(bits_down(size)):
        half = blocks.shape[0] // 2
        got = swap(blocks[half:], "ctx", bit)
        blocks = blocks[:half].astype(f32) + got.astype(f32)
        if half > 1:
            blocks = blocks.astype(bf16)
    return blocks[0]


def far_masks():
    return list(range(2, lax.axis_size("fsdp"), 2))


def gather_far(block):
    size = lax.axis_size("fsdp")
    masks = sorted(range(2, size, 2), key=lambda m: (m == size - 2, m == 2))
    far = {m: swap(block, "fsdp", m) for m in masks}
    return [block] + [far[m] for m in range(2, size, 2)]


def gather_near(pieces):
    out = []
    for piece in pieces:
        out += [piece, swap(piece, "fsdp", 1)]
    return out


def gather_fsdp(block):
    return gather_near(gather_far(block))


def scatter_first(even_a, odd_a, pairs_b):
    got = swap(odd_a, "fsdp", 1)
    sums_a = [even_a[i].astype(f32) + got[i].astype(f32) for i in range(even_a.shape[0])]
    sums_a = [sums_a[0]] + [part.astype(bf16) for part in sums_a[1:]]
    sum_b = pairs_b[0].astype(f32)
    for i, m in enumerate(far_masks()):
        sum_b = sum_b + swap(pairs_b[i + 1], "fsdp", m).astype(f32)
    return sums_a, sum_b[0], sum_b[1].astype(bf16)


def scatter_second(first, *others):
    sums_a, own_b, other_b = first
    total_a = sums_a[0]
    for i, m in enumerate(far_masks()):
        total_a = total_a + swap(after(sums_a[i + 1], *others), "fsdp", m).astype(f32)
    return total_a, own_b + swap(after(other_b, *others), "fsdp", 1).astype(f32)


def split_blocks(blocks, size):
    pairs = blocks.reshape(blocks.shape[0] // 2, 2, *blocks.shape[1:])
    parts_b = [pairs[i, :, :, size:] for i in range(pairs.shape[0])]
    return pairs[:, 0, :, :size], pairs[:, 1, :, :size], parts_b


def lane_chunk(values, flat):
    width = values.shape[1]
    row, lane = flat // width, flat % width
    return values[row : row + 1, lane : lane + LANES]


def at_block(block, width):
    return pl.ds(pl.multiple_of(block * width, LANES), width)


def rope(values, cosine, sine):
    return values * cosine + pltpu.roll(values, values.shape[1] // 2, 1) * sine


def rope_back(grads, cosine, sine):
    return grads * cosine + pltpu.roll(grads * sine, grads.shape[1] // 2, 1)


def over_blocks(block, carry, length, size):
    if length == size:
        return block(slice(0, size), carry)
    step = lambda i, kept: block(pl.ds(pl.multiple_of(i * size, size), size), kept)
    return lax.fori_loop(0, length // size, step, carry)


def out_kernel(f_ref, attn_ref, *refs):
    piece_refs, (own_ref, mixed_ref) = refs[:-2], refs[-2:]
    rows = piece_refs[0].shape[0]
    for q, piece_ref in enumerate(piece_refs):
        spot = pl.ds(pl.multiple_of(jnp.bitwise_xor(f_ref[0], q) * rows, rows), rows)
        own_ref[spot, :] = piece_ref[...]
    mixed_ref[...] = mm(attn_ref[...], own_ref[...]).astype(bf16)


def attend_kernel(sizes, f_ref, *refs):
    n_ctx, n_fsdp, head_dim, head_rows, norm_rows, q_rows = sizes
    x_refs, refs = refs[:n_ctx], refs[n_ctx:]
    w_refs, refs = refs[:n_fsdp], refs[n_fsdp:]
    cos_ref, sin_ref, dq_ref, dk_ref = refs[:4]
    a1_ref, qp_ref, kp_ref, q_ref, k_ref, v_ref, o_ref, gains_ref, heads_ref = refs[4:]
    f = f_ref[0]
    tok = x_refs[0].shape[0]
    length, width = q_ref.shape
    lane = lax.broadcasted_iota(jnp.int32, (8, LANES), 1)
    heads = [jnp.zeros((8, LANES), f32), jnp.zeros((8, LANES), f32)]
    for q in range(n_fsdp):
        block = jnp.bitwise_xor(f, q)
        extra = w_refs[q][3 * norm_rows :, :].astype(f32)
        for row in range(2):
            for k in range(norm_rows // LANES):
                spot = pl.ds(pl.multiple_of(block * norm_rows + k * LANES, LANES), LANES)
                gains_ref[row : row + 1, spot] = lane_chunk(extra, row * norm_rows + k * LANES)
            piece = jnp.broadcast_to(lane_chunk(extra, 2 * norm_rows + row * LANES), (8, LANES))
            piece = pltpu.roll(piece, block * head_rows, 1)
            heads[row] = jnp.where(lane // head_rows == block, piece, heads[row])
    for row in range(2):
        heads_ref[row : row + 1, :] = heads[row][:1]
    for i, x_ref in enumerate(x_refs):
        x = x_ref[...].astype(f32)
        a1_ref[i * tok : (i + 1) * tok, :] = rms_scale(x, gains_ref[0:1, :]).astype(bf16)
    outs = []
    for j in range(3):
        acc = None
        for q in range(n_fsdp):
            part = mm(
                a1_ref[:, at_block(jnp.bitwise_xor(f, q), norm_rows)],
                w_refs[q][j * norm_rows : (j + 1) * norm_rows, :],
            )
            acc = part if acc is None else acc + part
        if j == 0:
            qp_ref[...] = acc
        elif j == 1:
            kp_ref[...] = acc
        else:
            v_ref[...] = acc.astype(bf16)
    cosine, sine = cos_ref[...], sin_ref[...]
    for h in range(width // head_dim):
        cols = slice(h * head_dim, (h + 1) * head_dim)
        for from_ref, to_ref, row in ((qp_ref, q_ref, 0), (kp_ref, k_ref, 1)):
            normed = rms_scale(from_ref[:, cols], heads_ref[row : row + 1, :])
            to_ref[:, cols] = rope(normed, cosine, sine).astype(bf16)

        def block(rows, _):
            logits = mm(q_ref[rows, cols], k_ref[:, cols], NT) * head_dim**-0.5
            logits = jnp.where(dq_ref[rows, :] == dk_ref[...], logits, NEG_FILL)
            weights = jnp.exp(logits - jnp.max(logits, axis=1, keepdims=True))
            probs = weights * (1.0 / jnp.sum(weights, axis=1, keepdims=True))
            o_ref[rows, cols] = mm(probs.astype(bf16), v_ref[:, cols]).astype(bf16)
            return 0

        over_blocks(block, 0, length, q_rows)


def attend_back_kernel(sizes, *refs):
    n_ctx, head_dim, q_rows = sizes
    g_refs, refs = refs[:n_ctx], refs[n_ctx:]
    out_ref, q_ref, k_ref, v_ref, qp_ref, kp_ref, cos_ref, sin_ref, dq_ref, dk_ref, heads_ref = refs[:11]
    d_ref, hg_ref, go_ref = refs[11:]
    tok = g_refs[0].shape[0]
    length, width = q_ref.shape
    scale = head_dim**-0.5
    for i, g_ref in enumerate(g_refs):
        go_ref[i * tok : (i + 1) * tok, :] = mm(g_ref[...], out_ref[...], NT).astype(bf16)
    cosine, sine = cos_ref[...], sin_ref[...]
    sums = [None, None]
    for h in range(width // head_dim):
        cols = slice(h * head_dim, (h + 1) * head_dim)
        key, value = k_ref[:, cols], v_ref[:, cols]

        def block(rows, sums_of):
            d_key, d_value = sums_of
            query, d_out = q_ref[rows, cols], go_ref[rows, cols]
            logits = mm(query, key, NT) * scale
            logits = jnp.where(dq_ref[rows, :] == dk_ref[...], logits, NEG_FILL)
            weights = jnp.exp(logits - jnp.max(logits, axis=1, keepdims=True))
            probs = weights * (1.0 / jnp.sum(weights, axis=1, keepdims=True))
            d_prob = mm(d_out, value, NT)
            delta = jnp.sum(probs * d_prob, axis=1, keepdims=True)
            d_logit = (probs * (d_prob - delta)).astype(bf16)
            d_ref[0, rows, cols] = (mm(d_logit, key) * scale).astype(bf16)
            return (
                d_key + mm(d_logit, query, TN),
                d_value + mm(probs.astype(bf16), d_out, TN),
            )

        zeros = jnp.zeros((length, head_dim), f32)
        d_key, d_value = over_blocks(block, (zeros, zeros), length, q_rows)
        d_query = d_ref[0, :, cols].astype(f32)
        d_ref[2, :, cols] = d_value.astype(bf16)
        for row, grads, proj_ref in ((0, d_query, qp_ref), (1, d_key * scale, kp_ref)):
            grads = rope_back(grads.astype(bf16).astype(f32), cosine, sine)
            values = proj_ref[:, cols]
            root = lax.rsqrt(jnp.mean(values * values, axis=1, keepdims=True) + EPS)
            normed = values * root
            part = jnp.sum(grads * normed, axis=0, keepdims=True)
            sums[row] = part if sums[row] is None else sums[row] + part
            grads = grads * heads_ref[row : row + 1, :]
            inner = jnp.mean(grads * normed, axis=1, keepdims=True)
            d_ref[row, :, cols] = (root * (grads - normed * inner)).astype(bf16)
    for row in range(2):
        hg_ref[row : row + 1, :] = sums[row]


def project_back_kernel(sizes, f_ref, *refs):
    n_ctx, n_fsdp, head_rows, norm_rows = sizes
    x_refs, refs = refs[:n_ctx], refs[n_ctx:]
    w_refs, refs = refs[:n_fsdp], refs[n_fsdp:]
    a1_ref, d_ref, hg_ref, gain_two_ref = refs[:4]
    pay_refs, (da_ref, root_ref, extra_ref) = refs[4:-3], refs[-3:]
    pay_a, pay_b = pay_refs[:2], pay_refs[2:]
    f = f_ref[0]
    tok = x_refs[0].shape[0]
    width = d_ref.shape[2]
    for i, x_ref in enumerate(x_refs):
        x = x_ref[...].astype(f32)
        root_ref[i * tok : (i + 1) * tok, :] = lax.rsqrt(jnp.mean(x * x, axis=1, keepdims=True) + EPS)
    for q in range(n_fsdp):
        block = jnp.bitwise_xor(f, q)
        spot = at_block(block, norm_rows)
        flipped = a1_ref[:, spot].astype(f32).T.astype(bf16)
        da = None
        for j in range(3):
            rows = slice(j * norm_rows, (j + 1) * norm_rows)
            part = mm(d_ref[j], w_refs[q][rows, :], NT)
            da = part if da is None else da + part
            grad = mm(flipped, d_ref[j]).astype(bf16)
            if j == 2:
                pay_b[q // 2][q % 2, :norm_rows, :] = grad
            else:
                pay_a[q % 2][q // 2, rows, :] = grad
        da_ref[:, spot] = da.astype(bf16)
        gain = None
        for i, x_ref in enumerate(x_refs):
            rows = slice(i * tok, (i + 1) * tok)
            part = x_ref[:, spot].astype(f32) * root_ref[rows, :] * da[rows]
            part = jnp.sum(part, axis=0, keepdims=True)
            gain = part if gain is None else gain + part
        extra_ref[...] = jnp.zeros(extra_ref.shape, f32)
        for k in range(norm_rows // LANES):
            lanes = slice(k * LANES, (k + 1) * LANES)
            row, lane = k * LANES // width, k * LANES % width
            extra_ref[row : row + 1, lane : lane + LANES] = gain[:, lanes]
            two = norm_rows + k * LANES
            row, lane = two // width, two % width
            spot_two = pl.ds(pl.multiple_of(block * norm_rows + k * LANES, LANES), LANES)
            extra_ref[row : row + 1, lane : lane + LANES] = gain_two_ref[0:1, spot_two]
        for r in range(2):
            flat = 2 * norm_rows + r * LANES
            row, lane = flat // width, flat % width
            turned = jnp.broadcast_to(hg_ref[r : r + 1, :], (8, LANES))
            turned = pltpu.roll(turned, (n_fsdp - block) * head_rows, 1)
            extra_ref[row : row + 1, lane : lane + LANES] = turned[:1]
        pay_b[q // 2][q % 2, norm_rows:, :] = extra_ref[...].astype(bf16)


def finish_kernel(sizes, c_ref, *refs):
    n_ctx, norm_rows = sizes
    pay_refs, out_refs = refs[:n_ctx], refs[n_ctx : 2 * n_ctx]
    qkv_ref, out_ref = refs[2 * n_ctx :]
    c = c_ref[0]
    width = pay_refs[0].shape[1]
    piece_rows = out_refs[0].shape[0]
    for q in range(n_ctx):
        block = jnp.bitwise_xor(c, q)
        for j in range(3):
            rows = slice(j * norm_rows, (j + 1) * norm_rows)
            qkv_ref[j, :, at_block(block, width)] = pay_refs[q][rows, :].astype(f32)
        spot = pl.ds(pl.multiple_of(block * piece_rows, piece_rows), piece_rows)
        out_ref[spot, :] = out_refs[q][...].astype(f32)


def dispatch_kernel(picks_ref, scale_ref, *refs):
    piece_refs, dy_ref, all_ref = refs[:-2], refs[-2], refs[-1]
    tok = piece_refs[0].shape[0]

    @pl.when(pl.program_id(0) == 0)
    def _():
        for q, piece_ref in enumerate(reversed(piece_refs)):
            all_ref[q * tok : (q + 1) * tok, :] = piece_ref[...]

    dy_ref[0] = (mm(picks_ref[0], all_ref[...]) * scale_ref[0]).astype(bf16)


def hidden_kernel(picks_ref, dy_ref, wg_ref, wu_ref, wd_ref, *refs):
    piece_refs, (rows_ref, hid_ref, dg_ref, du_ref, all_ref) = refs[:-5], refs[-5:]
    tok = piece_refs[0].shape[0]
    first = pl.program_id(1) == 0

    @pl.when(first & (pl.program_id(0) == 0))
    def _():
        for q, piece_ref in enumerate(piece_refs):
            all_ref[q * tok : (q + 1) * tok, :] = piece_ref[...]

    @pl.when(first)
    def _():
        rows_ref[0] = mm(picks_ref[0], all_ref[...]).astype(bf16)

    rows = rows_ref[0]
    gate = mm(rows, wg_ref[0])
    up = mm(rows, wu_ref[0])
    d_hid = mm(dy_ref[0], wd_ref[0])
    sig = 1.0 / (1.0 + jnp.exp(-gate))
    act = gate * sig
    hid_ref[0] = (act * up).astype(bf16)
    dg_ref[0] = (d_hid * up * sig * (1.0 + gate * (1.0 - sig))).astype(bf16)
    du_ref[0] = (d_hid * act).astype(bf16)


def widen_kernel(from_ref, to_ref):
    to_ref[...] = from_ref[...].astype(f32)


def widen(values):
    count, rows, columns = values.shape
    block = pl.BlockSpec((1, min(rows, 256), columns), lambda i, j: (i, j, 0))
    return pl.pallas_call(
        widen_kernel,
        grid=(count, rows // min(rows, 256)),
        in_specs=[block],
        out_specs=block,
        out_shape=jax.ShapeDtypeStruct(values.shape, f32),
        compiler_params=params(24),
        cost_estimate=cost(5),
        name="widen",
    )(values)


def body(
    inputs,
    doc_starts,
    routes,
    gate_weights,
    qkv_w,
    out_w,
    norm_gains,
    head_gains,
    gate_up,
    down_t,
    cotangent,
):
    n_ctx, n_fsdp = lax.axis_size("ctx"), lax.axis_size("fsdp")
    c, f = lax.axis_index("ctx"), lax.axis_index("fsdp")
    c_at, f_at = c.astype(jnp.int32).reshape(1), f.astype(jnp.int32).reshape(1)
    tok_rows, model_width = inputs.shape[1:]
    norm_rows, head_rows = norm_gains.shape[0], head_gains.shape[0]
    head_dim = head_rows * n_fsdp
    own_width = model_width // n_ctx
    top_count = routes.shape[2]
    hidden_units = down_t.shape[2]
    local_experts = gate_up.shape[1]
    experts_all = local_experts * n_fsdp
    capacity = tok_rows * top_count * 5 // (experts_all * 4)
    slots = -(-n_fsdp * capacity // 16) * 16
    stream_len = doc_starts.shape[1]
    q_rows = min(512, stream_len)
    half_dim = head_dim // 2
    tokens = n_fsdp * tok_rows
    order = folded_order(n_ctx)

    x_low = inputs[0]
    x_rows = x_low.astype(f32)
    cot_low = cotangent[0]
    cot_rows = cot_low.astype(f32)

    weights = gate_weights[0].T.reshape(-1)
    high = lax.reduce_precision(weights, 8, 7)
    middle = lax.reduce_precision(weights - high, 8, 7)
    gap = jnp.zeros((LANES - head_rows,), bf16)
    small = jnp.concatenate(
        [
            norm_gains.T.reshape(-1),
            head_gains[:, 0],
            gap,
            head_gains[:, 1],
            gap,
            routes[0].T.reshape(-1).astype(bf16),
            high.astype(bf16),
            middle.astype(bf16),
            (weights - high - middle).astype(bf16),
        ]
    )
    extra_rows = -(-small.shape[0] // (16 * own_width)) * 16
    small = jnp.pad(small, (0, extra_rows * own_width - small.shape[0]))
    qkv_own = lax.dynamic_slice_in_dim(qkv_w, c * own_width, own_width, axis=2)
    qkv_own = qkv_own.transpose(1, 0, 2).reshape(3 * norm_rows, own_width)
    qkv_own = jnp.concatenate([qkv_own, small.reshape(extra_rows, own_width)], axis=0)
    qkv_pieces = gather_fsdp(qkv_own)

    x_pieces = gather_ctx(x_low)
    x_pieces = [x_pieces[q] for q in order]

    units = n_ctx * n_fsdp
    out_rows = out_w.shape[0] // n_ctx
    flat = lambda ci, fi: ci * n_fsdp + fi
    to_heads = [(flat(u % n_ctx, u // n_ctx), flat(u // n_fsdp, u % n_fsdp)) for u in range(units)]
    out_piece = lax.dynamic_slice_in_dim(out_w, c * out_rows, out_rows, axis=0)
    out_piece = lax.ppermute(after(out_piece, *x_pieces), ("ctx", "fsdp"), to_heads)
    split = model_width * 11 // (16 * LANES) * LANES
    out_far = gather_far(after(out_piece, qkv_pieces[-1]))
    out_pieces = gather_near(out_far)

    cot_far = gather_far(after(cot_low, *out_far))
    gate_up_all = lax.all_gather(gate_up.transpose(1, 0, 2), "ctx", axis=1, tiled=True)
    down_all = lax.all_gather(
        down_t.transpose(1, 0, 2), "ctx", axis=1, tiled=True
    )

    places = jnp.arange(stream_len, dtype=jnp.int32)
    blocks = jnp.repeat(jnp.asarray(order, jnp.int32), tok_rows)
    spots = (c ^ blocks) * tok_rows + places % tok_rows
    starts = doc_starts[0]
    reach = spots[:, None] >= places[None, :]
    doc_ids = jnp.sum(jnp.where(reach, starts[None, :], 0), axis=1)
    begins = jnp.max(jnp.where(reach & (starts[None, :] == 1), places[None, :], 0), axis=1)
    relative = spots - begins
    frequency = jnp.exp(jnp.arange(half_dim, dtype=f32) * (-2.0 / head_dim) * math.log(ROPE_BASE))
    angles = relative.astype(f32)[:, None] * frequency[None, :]
    cosine = jnp.cos(angles)
    cosine = jnp.concatenate([cosine, cosine], axis=1)
    sine = jnp.sin(angles)
    sine = jnp.concatenate([-sine, sine], axis=1)
    doc_q, doc_k = doc_ids[:, None], doc_ids[None, :]

    act = jax.ShapeDtypeStruct((stream_len, own_width), bf16)
    wide = jax.ShapeDtypeStruct((stream_len, own_width), f32)
    a1, q_proj, k_proj, q_low, k_low, v_low, attn_low, gains, heads = pl.pallas_call(
        functools.partial(
            attend_kernel, (n_ctx, n_fsdp, head_dim, head_rows, norm_rows, q_rows)
        ),
        in_specs=[SMEM] + [VMEM] * (n_ctx + n_fsdp + 4),
        out_specs=[VMEM] * 9,
        out_shape=[
            jax.ShapeDtypeStruct((stream_len, model_width), bf16),
            wide,
            wide,
            act,
            act,
            act,
            act,
            jax.ShapeDtypeStruct((2, model_width), f32),
            jax.ShapeDtypeStruct((2, head_dim), f32),
        ],
        compiler_params=params(48),
        cost_estimate=cost(1),
        name="attend",
    )(f_at, *x_pieces, *qkv_pieces, cosine, sine, doc_q, doc_k)
    out_own, mixed_heads = pl.pallas_call(
        out_kernel,
        in_specs=[SMEM] + [VMEM] * (n_fsdp + 1),
        out_specs=[VMEM] * 2,
        out_shape=[
            jax.ShapeDtypeStruct((own_width, model_width), bf16),
            jax.ShapeDtypeStruct((stream_len, model_width), bf16),
        ],
        compiler_params=params(40),
        cost_estimate=cost(1),
        name="out",
    )(f_at, attn_low, *out_pieces)
    h_one = x_rows + scatter_ctx(mixed_heads.reshape(n_ctx, tok_rows, model_width))
    a2_f32, norm_two_back = jax.vjp(rms_scale, h_one, gains[1])
    a2_low = a2_f32.astype(bf16)
    a2_pieces = gather_fsdp(a2_low)
    cot_pieces = gather_near([after(piece, a2_low) for piece in cot_far])

    extras = jnp.stack([piece[3 * norm_rows :].reshape(-1) for piece in qkv_pieces]).astype(f32)
    route_at = 2 * norm_rows + 2 * LANES
    count = tok_rows * top_count
    spread = extras[:, route_at : route_at + 4 * count].reshape(n_fsdp, 4, top_count, tok_rows)
    spread = spread.transpose(1, 2, 0, 3).reshape(4, top_count, tokens)
    own = (f * local_experts + jnp.arange(local_experts, dtype=jnp.int32)).astype(f32)
    chosen = spread[0][None] == own[:, None, None]
    token_weight = spread[1] + spread[2] + spread[3]
    member = jnp.any(chosen, axis=1)
    weight = jnp.sum(jnp.where(chosen, token_weight[None], 0.0), axis=1)
    token_ids = jnp.arange(tokens, dtype=jnp.int32)
    before = (token_ids[:, None] < token_ids[None, :]).astype(bf16)
    rank = mm(member.astype(bf16), before).astype(jnp.int32)
    place = jnp.where(member, rank, -1)
    slot_ids = jnp.arange(slots, dtype=jnp.int32)
    picks = place[:, None, :] == slot_ids[None, :, None]
    scale = jnp.sum(jnp.where(picks, weight[:, None, :], 0.0), axis=2, keepdims=True)
    picks = picks.astype(bf16)
    tile = 512
    per_expert = lambda *shape: pl.BlockSpec((1,) + shape, lambda e, j: (e, 0, 0))
    whole = lambda *shape: pl.BlockSpec(shape, lambda *_: (0,) * len(shape))
    column = lambda rows_of, shift: pl.BlockSpec((1, rows_of, tile), lambda e, j: (e, 0, j + shift))
    piece_specs = [whole(tok_rows, model_width)] * n_fsdp
    row_shape = jax.ShapeDtypeStruct((local_experts, slots, model_width), bf16)
    gathered = [pltpu.VMEM((tokens, model_width), bf16)]
    dy = pl.pallas_call(
        dispatch_kernel,
        grid=(local_experts,),
        in_specs=[
            pl.BlockSpec((1, slots, tokens), lambda e: (e, 0, 0)),
            pl.BlockSpec((1, slots, 1), lambda e: (e, 0, 0)),
        ]
        + piece_specs,
        out_specs=pl.BlockSpec((1, slots, model_width), lambda e: (e, 0, 0)),
        out_shape=row_shape,
        scratch_shapes=gathered,
        compiler_params=params(40),
        cost_estimate=cost(5),
        name="dispatch",
    )(picks, scale, *reversed(cot_pieces))
    hid_shape = jax.ShapeDtypeStruct((local_experts, slots, hidden_units), bf16)
    rows, hidden_low, gate_grad, up_grad = pl.pallas_call(
        hidden_kernel,
        grid=(local_experts, hidden_units // tile),
        in_specs=[
            per_expert(slots, tokens),
            per_expert(slots, model_width),
            column(model_width, 0),
            column(model_width, hidden_units // tile),
            column(model_width, 0),
        ]
        + piece_specs,
        out_specs=[per_expert(slots, model_width)] + [column(slots, 0)] * 3,
        out_shape=[
            row_shape,
            hid_shape,
            hid_shape,
            hid_shape,
        ],
        scratch_shapes=gathered,
        compiler_params=params(48),
        cost_estimate=cost(20),
        name="hidden",
    )(picks, dy, gate_up_all, gate_up_all, down_all, *a2_pieces)

    pair_grad = jnp.concatenate([gate_grad, up_grad], axis=2)

    token_blocks = lambda values: split_blocks(values.reshape(n_fsdp, tok_rows, model_width), split)
    down_part = jnp.einsum("erd,erf->edf", dy, hidden_low, preferred_element_type=f32).astype(bf16)
    down_grad = widen(lax.psum_scatter(down_part, "ctx", scatter_dimension=1, tiled=True))
    dxe = jnp.einsum("erk,edk->erd", after(pair_grad, down_part), gate_up_all, preferred_element_type=f32).astype(bf16)
    grads_back = jnp.einsum("est,esd->td", picks, dxe, preferred_element_type=f32).astype(bf16)
    dx_first = scatter_first(*token_blocks(grads_back))
    pair_part = jnp.einsum(
        "erd,erk->edk", after(rows, grads_back), pair_grad, preferred_element_type=f32
    ).astype(bf16)
    gate_up_grad = widen(lax.psum_scatter(pair_part, "ctx", scatter_dimension=1, tiled=True))
    da2 = jnp.concatenate(scatter_second(dx_first, pair_part), axis=1)
    made = jnp.einsum(
        "erf,edf->erd", after(hidden_low, *dx_first[0], *dx_first[1:]), down_all, preferred_element_type=f32
    )
    made = (scale * made.astype(bf16).astype(f32)).astype(bf16)
    mixed = jnp.einsum("est,esd->td", picks, made, preferred_element_type=f32).astype(bf16)
    mixed_first = scatter_first(*token_blocks(mixed))

    dh_part, gain_two_grad = norm_two_back(da2)
    dh_one = cot_rows + dh_part
    dattn_pieces = gather_ctx(after(dh_one.astype(bf16), mixed))
    dattn_pieces = [dattn_pieces[q] for q in order]
    proj_grad, head_grads = pl.pallas_call(
        functools.partial(attend_back_kernel, (n_ctx, head_dim, q_rows)),
        in_specs=[VMEM] * (n_ctx + 11),
        out_specs=[VMEM] * 2,
        out_shape=[
            jax.ShapeDtypeStruct((3, stream_len, own_width), bf16),
            jax.ShapeDtypeStruct((2, head_dim), f32),
        ],
        scratch_shapes=[pltpu.VMEM((stream_len, own_width), bf16)],
        compiler_params=params(56),
        cost_estimate=cost(500),
        name="attend_back",
    )(*dattn_pieces, out_own, q_low, k_low, v_low, q_proj, k_proj, cosine, sine, doc_q, doc_k, heads)
    dattn = jnp.concatenate(dattn_pieces, axis=0)
    out_part = mm(attn_low, dattn, TN).astype(bf16)
    out_blocks = jnp.stack(
        [
            lax.dynamic_slice_in_dim(out_part, (f ^ q) * out_rows, out_rows, axis=0)
            for q in range(n_fsdp)
        ]
    )
    out_first_sums = scatter_first(*split_blocks(out_blocks, split))
    half_stack = jax.ShapeDtypeStruct((n_fsdp // 2, 2 * norm_rows, own_width), bf16)
    pair_shape = jax.ShapeDtypeStruct((2, norm_rows + extra_rows, own_width), bf16)
    even_a, odd_a, *pairs_b, da1 = pl.pallas_call(
        functools.partial(project_back_kernel, (n_ctx, n_fsdp, head_rows, norm_rows)),
        in_specs=[SMEM] + [VMEM] * (n_ctx + n_fsdp + 4),
        out_specs=[VMEM] * (n_fsdp // 2 + 3),
        out_shape=[half_stack] * 2
        + [pair_shape] * (n_fsdp // 2)
        + [jax.ShapeDtypeStruct((stream_len, model_width), bf16)],
        scratch_shapes=[
            pltpu.VMEM((stream_len, 1), f32),
            pltpu.VMEM((extra_rows, own_width), f32),
        ],
        compiler_params=params(56),
        cost_estimate=cost(10),
        name="project_back",
    )(f_at, *x_pieces, *qkv_pieces, a1, proj_grad, head_grads, gain_two_grad[None])
    ready = (*mixed_first[0], *mixed_first[1:], *out_first_sums[0], *out_first_sums[1:])
    payload_first = scatter_first(even_a, after(odd_a, *ready), pairs_b)
    da1 = scatter_ctx(da1.reshape(n_ctx, tok_rows, model_width))
    payload_parts = scatter_second(payload_first, down_grad)
    qkv_sum = jnp.concatenate(payload_parts, axis=0)
    out_parts = scatter_second(out_first_sums, *payload_parts)
    out_sum = jnp.concatenate(out_parts, axis=1)
    out_sum = lax.ppermute(out_sum.astype(bf16), ("ctx", "fsdp"), [(b, a) for a, b in to_heads])
    out_ends = gather_ctx(out_sum)
    _, norm_one_back = jax.vjp(lambda x: rms_scale(x, gains[0]), x_rows)
    inputs_grad = dh_one + norm_one_back(da1)[0]
    ends = gather_ctx(after(qkv_sum.astype(bf16), da1))
    qkv_grad, out_grad = pl.pallas_call(
        functools.partial(finish_kernel, (n_ctx, norm_rows)),
        in_specs=[SMEM] + [VMEM] * (2 * n_ctx),
        out_specs=[VMEM] * 2,
        out_shape=[
            jax.ShapeDtypeStruct((3, norm_rows, model_width), f32),
            jax.ShapeDtypeStruct((norm_rows, model_width), f32),
        ],
        compiler_params=params(40),
        cost_estimate=cost(1),
        name="finish",
    )(c_at, *ends, *out_ends)
    mixed_first[0][0] = after(mixed_first[0][0], gate_up_grad)
    mixed_parts = scatter_second(mixed_first, *payload_parts)
    block_out = (h_one + jnp.concatenate(mixed_parts, axis=1)).astype(bf16)
    extras = sum(piece[3 * norm_rows :].astype(f32) for piece in ends).reshape(-1)
    norm_grad = extras[: 2 * norm_rows].reshape(2, norm_rows).T
    head_grad = extras[2 * norm_rows : route_at].reshape(2, LANES)[:, :head_rows].T
    return (
        block_out[None],
        inputs_grad[None],
        qkv_grad.transpose(1, 0, 2),
        out_grad,
        norm_grad,
        head_grad,
        gate_up_grad.transpose(1, 0, 2),
        down_grad.transpose(1, 0, 2),
    )


def solution(mesh):
    return jax.shard_map(
        body,
        mesh=mesh,
        in_specs=(
            P("fsdp", "ctx", None),
            P("fsdp", None),
            P("fsdp", "ctx", None),
            P("fsdp", "ctx", None),
            P("fsdp", None, None),
            P("fsdp", None),
            P("fsdp", None),
            P("fsdp", None),
            P("ctx", "fsdp", None),
            P("ctx", "fsdp", None),
            P("fsdp", "ctx", None),
        ),
        out_specs=(
            P("fsdp", "ctx", None),
            P("fsdp", "ctx", None),
            P("fsdp", None, None),
            P("fsdp", None),
            P("fsdp", None),
            P("fsdp", None),
            P("ctx", "fsdp", None),
            P("ctx", "fsdp", None),
        ),
        check_vma=False,
    )
```
